128 devices in a mesh: dp: 16 (over y, x), tensor: 8 (over z, core).
Axes of the slice: x: 4, y: 4, z: 4, core: 2. Of those that a mesh axis runs over, the one named last changes fastest.
Arguments:
- old_master: float32 [128, 672, 128], P(('dp', 'tensor')), may hold values from -6 to 6
- old_avg: float32 [128, 672, 128], P(('dp', 'tensor')), may hold values from -1.8 to 1.8
- old_sq: float32 [128, 672, 128], P(('dp', 'tensor')), may hold values from 0.001 to 1
- grad: float32 [128, 672, 128], P(('dp', 'tensor')), may hold values from -6 to 6
- old_table: int32 [128, 3], replicated, may hold values from 0 to 10751, as said below
- new_table: int32 [128, 3], replicated, may hold values from 0 to 5375, as said below
- head_order: int32 [112], replicated, may hold values from 0 to 111, each once
Outputs:
- new_master: float32 [128, 672, 128], P(('dp', 'tensor'))
- new_avg: float32 [128, 672, 128], P(('dp', 'tensor'))
- new_sq: float32 [128, 672, 128], P(('dp', 'tensor'))
- params: bfloat16 [128, 43008], P(None, 'tensor')
The draws below stay inside these ranges and needn't reach their ends.
Inputs may be any that keep to these rules, and one draw needn't show every extreme that they name: `old_table`: row k belongs to old rank k // 32; the fragments of one old rank follow one another in k without gaps and cover its 10752 units; every length is 1 to 672, in each old rank one length is exactly 672, and the last fragment of each old rank has length 1. `new_table`: row k = d * 8 + n belongs to new rank n; for one new rank the ranges follow one another in d without gaps and cover its 5376 units; range d lies within units d * 336 to (d + 3) * 336 - 1; every length is 1 to 672, in each new rank one length is exactly 672 and that range reaches unit (d + 2) * 336 or beyond, and the last range of each new rank has length 1.
All inputs are finite; a program needn't handle non-finite values.
Results may differ from the reference program's by a relative error of at most 0.0033.
Values may be sent and summed in bfloat16 or wider, within the bound.
No kernel may reach another device: no remote copies, remote signals or barrier semaphores. Data moves between devices by JAX's collectives and lax.ppermute only.
A program may use at most 128 MiB of HBM per device.

```python
import math
import jax
import jax.numpy as jnp
from jax import lax

HEADS = 112
HDIM = 128
OLD_TP = 4
STEPS_DONE = 10
ROWS = 128
UNIT_DEV = 336
SLOT = 672
N_DP = 16
N_TENSOR = 8
DEVICES = 128


def ragged_lengths(key, rank_count, frag_count, typical):
    key_small, key_place = jax.random.split(key)
    middle = jax.random.randint(key_small, (rank_count, frag_count), 1, typical, dtype=jnp.int32)
    chosen = jax.random.randint(key_place, (rank_count, 1), 0, frag_count - 2, dtype=jnp.int32)
    column = jnp.arange(frag_count, dtype=jnp.int32)[None, :]
    middle = jnp.where(column == chosen, typical, middle)
    middle = jnp.where(column == (chosen - 1) % frag_count, 0, middle)
    middle = jnp.where(column == frag_count - 2, typical - 1, middle)
    middle = jnp.where(column == frag_count - 1, 0, middle)
    return (typical + middle - jnp.roll(middle, 1, axis=1)).astype(jnp.int32)


def draw_old_table(key, part):
    key = jax.random.fold_in(key, 11)
    frag_count = DEVICES // OLD_TP
    lengths = ragged_lengths(key, OLD_TP, frag_count, UNIT_DEV)
    ordered = jnp.sort(lengths[:, :frag_count - 1], axis=1)
    lengths = jnp.concatenate([ordered, lengths[:, frag_count - 1:]], axis=1).astype(jnp.int32)
    starts = jnp.cumsum(lengths, axis=1) - lengths
    ranks = jnp.broadcast_to(jnp.arange(OLD_TP, dtype=jnp.int32)[:, None], (OLD_TP, frag_count))
    table = jnp.stack([ranks.reshape(-1), starts.reshape(-1), lengths.reshape(-1)], axis=1)
    return table.astype(jnp.int32)


def draw_new_table(key, part):
    key = jax.random.fold_in(key, 23)
    typical = UNIT_DEV
    key_small, key_place = jax.random.split(key)
    middle = jax.random.randint(key_small, (N_TENSOR, N_DP), 1, typical, dtype=jnp.int32)
    chosen = jax.random.randint(key_place, (N_TENSOR, 1), 1, N_DP - 2, dtype=jnp.int32)
    column = jnp.arange(N_DP, dtype=jnp.int32)[None, :]
    middle = jnp.where(column == chosen - 1, typical // 2, middle)
    middle = jnp.where(column == chosen, typical + typical // 2, middle)
    middle = jnp.where(column == chosen + 1, typical - 1, middle)
    middle = jnp.where(column == N_DP - 2, typical - 1, middle)
    middle = jnp.where(column == N_DP - 1, 0, middle)
    lengths = (typical + middle - jnp.roll(middle, 1, axis=1)).astype(jnp.int32)
    starts = jnp.cumsum(lengths, axis=1) - lengths
    ranks = jnp.broadcast_to(jnp.arange(N_TENSOR, dtype=jnp.int32)[:, None], (N_TENSOR, N_DP))
    table = jnp.stack([ranks, starts, lengths], axis=2)
    return table.transpose(1, 0, 2).reshape(DEVICES, 3).astype(jnp.int32)


def steps_of(stream_key, shape, cuts, least, high):
    def one(position, blocks):
        steps = jax.random.uniform(jax.random.fold_in(jax.random.fold_in(stream_key, 6), position), (blocks,), jnp.float32, least / len(cuts), high / len(cuts))
        return jnp.repeat(jnp.exp(steps), shape[position] // blocks).reshape((-1,) + (1,) * (len(shape) - position - 1))

    factor_of = one(*cuts[0])
    for cut in cuts[1:]:
        factor_of = factor_of * one(*cut)
    return factor_of


def gaussian(key, extent, spread, reach, cuts=(), held_as=jnp.bfloat16):
    level = steps_of(key, extent, cuts, -0.22, 0.18) if cuts else 1.0
    entries = jax.random.normal(key, extent, jnp.float32) * spread * level
    return jnp.minimum(jnp.maximum(entries, -reach), reach).astype(held_as)


def setup_inputs(seed: int = 0) -> dict:
    key_of = jax.random.split(jax.random.key(seed), 8)
    old_master = gaussian(key_of[0], (DEVICES, SLOT, HDIM), 1.0, 6.0, ((0, 128),), jnp.float32)
    old_avg = gaussian(key_of[1], (DEVICES, SLOT, HDIM), 0.3, 1.8, ((0, 128),), jnp.float32)
    old_sq = jnp.clip(jnp.exp(math.log(1.0) - 6.9077552 * jax.random.uniform(key_of[2], (DEVICES, SLOT, HDIM), jnp.float32) ** steps_of(key_of[2], (DEVICES, SLOT, HDIM), ((0, 128),), -0.2, 0.2)), 0.001, 1.0)
    grad = gaussian(key_of[3], (DEVICES, SLOT, HDIM), 1.0, 6.0, ((0, 128),), jnp.float32)
    old_table = draw_old_table(jax.random.fold_in(key_of[7], 71), 0)
    new_table = draw_new_table(jax.random.fold_in(key_of[7], 71), 0)
    head_order = jax.random.permutation(key_of[6], HEADS).astype(jnp.int32)
    return dict(old_master=old_master, old_avg=old_avg, old_sq=old_sq, grad=grad, old_table=old_table, new_table=new_table, head_order=head_order)


beta_first = 0.9
beta_second = 0.95
learn_rate = 0.1
decay_rate = 0.1
epsilon_add = 1e-08

def adam_update(master, moment, square, gradient):
    moment_new = beta_first * moment + (1.0 - beta_first) * gradient
    square_new = beta_second * square + (1.0 - beta_second) * gradient * gradient
    moment_hat = moment_new / (1.0 - beta_first ** STEPS_DONE)
    square_hat = square_new / (1.0 - beta_second ** STEPS_DONE)
    master_new = master - learn_rate * (moment_hat / (jnp.sqrt(square_hat) + epsilon_add) + decay_rate * master)
    return (master_new, moment_new, square_new)

def assemble(pieces, table, rank, total):
    place = jnp.arange(total, dtype=jnp.int32)
    begin = table[:, 1][:, None]
    covered = (table[:, 0][:, None] == rank) & (begin <= place[None, :]) & (place[None, :] < begin + table[:, 2][:, None])
    rows_ids = jnp.arange(table.shape[0], dtype=jnp.int32)[:, None]
    owner = lax.optimization_barrier(jnp.sum(jnp.where(covered, rows_ids, 0), axis=0)).astype(jnp.int32)
    offset = (place - table[owner, 1]).astype(jnp.int32)
    return pieces[owner, offset]

def reference(old_master, old_avg, old_sq, grad, old_table, new_table, head_order):
    heads_old = HEADS // OLD_TP
    heads_new = HEADS // N_TENSOR
    old_total = ROWS * 3 * heads_old
    new_total = ROWS * 3 * heads_new

    def rebuild(pieces):
        per_rank = [assemble(pieces, old_table, rank, old_total).reshape(ROWS, heads_old, 3, HDIM) for rank in range(OLD_TP)]
        weight = jnp.concatenate(per_rank, axis=1)
        moved = weight[:, head_order].reshape(ROWS, N_TENSOR, heads_new, 3, HDIM)
        return moved.transpose(1, 0, 3, 2, 4).reshape(N_TENSOR, new_total, HDIM)
    masters = rebuild(old_master)
    moments = rebuild(old_avg)
    squares = rebuild(old_sq)
    gradients = jnp.stack([assemble(grad, new_table, rank, new_total) for rank in range(N_TENSOR)])
    master_new, moment_new, square_new = adam_update(masters, moments, squares, gradients)
    place = jnp.arange(SLOT, dtype=jnp.int32)
    rank_of = new_table[:, 0][:, None]
    index = jnp.clip(new_table[:, 1][:, None] + place[None, :], 0, new_total - 1).astype(jnp.int32)
    inside = (place[None, :] < new_table[:, 2][:, None])[:, :, None]

    def owned(flat):
        return jnp.where(inside, flat[rank_of, index], 0.0)
    weights = master_new.reshape(N_TENSOR, ROWS, 3 * heads_new * HDIM).transpose(1, 0, 2)
    params = weights.reshape(ROWS, 3 * HEADS * HDIM).astype(jnp.bfloat16)
    return (owned(master_new), owned(moment_new), owned(square_new), params)
```

```python
import functools
import jax
import jax.numpy as jnp
from jax import lax
from jax.experimental import pallas as pl
from jax.experimental.pallas import tpu as pltpu
from jax.sharding import Mesh, PartitionSpec as P

OLD_TP = 4
STEPS_DONE = 10
SLOT = 672
UNIT = 336
LANES = 128
ROW_OLD = 84
QUART = 21
QPAD = 24
ROW_NEW = 42
RPAD = 48

beta_first = 0.9
beta_second = 0.95
learn_rate = 0.1
decay_rate = 0.1
epsilon_add = 1e-08

SCALE_W = 2.0**13
SCALE_M = 2.0**15
SCALE_V = 2.0**15
SCALE_G = 2.0**13


def adam_update(master, moment, square, gradient):
    moment_new = beta_first * moment + (1.0 - beta_first) * gradient
    square_new = beta_second * square + (1.0 - beta_second) * gradient * gradient
    moment_hat = moment_new / (1.0 - beta_first**STEPS_DONE)
    square_hat = square_new / (1.0 - beta_second**STEPS_DONE)
    master_new = master - learn_rate * (
        moment_hat / (jnp.sqrt(square_hat) + epsilon_add) + decay_rate * master
    )
    return (master_new, moment_new, square_new)


def wrap(value):
    return jnp.where(value < 0, value + SLOT, value)


def pack_kernel(place, w_ref, m_ref, v_ref, g_ref, out_ref, gout_ref, scratch):
    for s, ref in enumerate((w_ref, m_ref, v_ref, g_ref)):
        scratch[s, pl.ds(0, SLOT), :] = ref[0]
        scratch[s, pl.ds(SLOT, RPAD), :] = ref[0, pl.ds(0, RPAD), :]
    scales = (SCALE_W, SCALE_M, SCALE_V)
    for hq in range(4):
        for t in range(8):
            offset = wrap(t * ROW_OLD + hq * QUART - place[0])
            for s in range(3):
                piece = scratch[s, pl.ds(offset, QPAD), :]
                out_ref[hq * 8 + t, :, pl.ds(s * LANES, LANES)] = piece * scales[s]
    for half in range(2):
        for t in range(8):
            offset = wrap(half * UNIT + t * ROW_NEW - place[1])
            gout_ref[half, t] = scratch[3, pl.ds(offset, RPAD), :] * SCALE_G


def owner_kernel(place, near_ref, mid_ref, g_ref, w_out, m_out, v_out, scratch):
    for half, ref in enumerate((near_ref, mid_ref)):
        for t in range(8):
            for s in range(3):
                piece = ref[t, pl.ds(0, ROW_NEW), pl.ds(s * LANES, LANES)]
                at = half * UNIT + t * ROW_NEW
                scratch[s, pl.ds(at, ROW_NEW), :] = piece
                scratch[s, pl.ds(at + SLOT, ROW_NEW), :] = piece
    step = 96
    for c in range(SLOT // step):
        at = place[1] + c * step
        w = scratch[0, pl.ds(at, step), :] * (1.0 / SCALE_W)
        m = scratch[1, pl.ds(at, step), :] * (1.0 / SCALE_M)
        v = scratch[2, pl.ds(at, step), :] * (1.0 / SCALE_V)
        rows = pl.ds(c * step, step)
        slot = lax.broadcasted_iota(jnp.int32, (step, LANES), 0) + c * step
        inside = slot < place[2]
        new = adam_update(w, m, v, g_ref[0, rows, :])
        for ref, value in zip((w_out, m_out, v_out), new):
            ref[0, rows, :] = jnp.where(inside, value, 0.0)


def one_hot_dot(chosen, source):
    picked = jnp.dot(
        chosen.astype(jnp.float32),
        source.astype(jnp.float32),
        precision=lax.Precision.HIGH,
        preferred_element_type=jnp.float32,
    )
    return picked.astype(jnp.float16)


def on_device(old_master, old_avg, old_sq, grad, old_table, new_table, head_order):
    y = lax.axis_index("y")
    x = lax.axis_index("x")
    t = lax.axis_index("tensor")
    dp = y * 4 + x
    dev = dp * 8 + t
    f16 = jnp.float16

    new_start = new_table[dev, 1]
    new_length = new_table[dev, 2]
    place = jnp.stack(
        [
            old_table[dev, 1] % SLOT,
            (new_start - dp * UNIT) % SLOT,
            new_length,
        ]
    ).astype(jnp.int32)

    vmem = pl.BlockSpec(memory_space=pltpu.VMEM)
    smem = pl.BlockSpec(memory_space=pltpu.SMEM)
    packed, grad_rows = pl.pallas_call(
        pack_kernel,
        out_shape=(
            jax.ShapeDtypeStruct((32, QPAD, 3 * LANES), jnp.float32),
            jax.ShapeDtypeStruct((2, 8, RPAD, LANES), jnp.float32),
        ),
        in_specs=[smem, vmem, vmem, vmem, vmem],
        out_specs=(vmem, vmem),
        scratch_shapes=[pltpu.VMEM((4, SLOT + RPAD, LANES), jnp.float32)],
        compiler_params=pltpu.CompilerParams(vmem_limit_bytes=24 * 1024 * 1024),
    )(place, old_master, old_avg, old_sq, grad)

    grad_send = grad_rows.astype(f16)
    up = lambda by: [(i, i + by) for i in range(16 - by)]
    down = lambda by: [(i + by, i) for i in range(16 - by)]
    grad_one = lax.ppermute(grad_send[1], ("y", "x"), up(1))
    grad_two = lax.ppermute(grad_send[0], ("y", "x"), up(2))

    first = lax.all_to_all(packed.astype(f16), ("x", "tensor"), 0, 0, tiled=True)
    ranks = lax.dynamic_slice_in_dim(old_table, y * 32, 32, 0)
    begin = jnp.broadcast_to(ranks[:, 1:2], (32, QPAD)).reshape(1, 32 * QPAD)
    end = begin + jnp.broadcast_to(ranks[:, 2:3], (32, QPAD)).reshape(1, 32 * QPAD)
    row_id = lax.broadcasted_iota(jnp.int32, (16 * QPAD, 32 * QPAD), 0)
    col_id = lax.broadcasted_iota(jnp.int32, (16 * QPAD, 32 * QPAD), 1)
    j = row_id % QPAD
    flat = ((row_id // QPAD) * 8 + t) * ROW_OLD + x * QUART + j
    chosen = (j == col_id % QPAD) & (j < QUART) & (flat >= begin) & (flat < end)
    rows = one_hot_dot(chosen, first.reshape(32 * QPAD, 3 * LANES))

    second = lax.all_to_all(
        rows.reshape(16, QPAD, 3 * LANES), ("y", "x"), 0, 0, tiled=True
    )
    order = head_order.reshape(8, 1, 14)
    comp = jnp.arange(3, dtype=jnp.int32).reshape(1, 3, 1)
    origin = (order // 7) * QPAD + (order % 7) * 3 + comp
    origin = jnp.pad(origin.reshape(8, ROW_NEW), ((0, 0), (0, RPAD - ROW_NEW)))
    origin = origin.reshape(8 * RPAD, 1)
    col_id = lax.broadcasted_iota(jnp.int32, (8 * RPAD, 16 * QPAD), 1)
    heads = one_hot_dot(origin == col_id, second.reshape(16 * QPAD, 3 * LANES))

    block = lax.all_to_all(heads.reshape(8, RPAD, 3 * LANES), "tensor", 0, 0, tiled=True)
    block_one = lax.ppermute(block, ("y", "x"), down(1))
    block_two = lax.ppermute(block, ("y", "x"), down(2))

    own = lax.broadcasted_iota(jnp.int32, (8, RPAD, 1), 0) * ROW_NEW
    own = own + lax.broadcasted_iota(jnp.int32, (8, RPAD, 1), 1) + dp * UNIT
    start_below = new_table[jnp.maximum(dp - 1, 0) * 8 + t, 1]
    gradient = jnp.where(
        own >= new_start,
        grad_send[0].astype(jnp.float32),
        jnp.where(
            own >= start_below, grad_one.astype(jnp.float32), grad_two.astype(jnp.float32)
        ),
    ) * (1.0 / SCALE_G)
    wide = block.astype(jnp.float32)
    master, _, _ = adam_update(
        wide[:, :, :LANES] * (1.0 / SCALE_W),
        wide[:, :, LANES : 2 * LANES] * (1.0 / SCALE_M),
        wide[:, :, 2 * LANES :] * (1.0 / SCALE_V),
        gradient,
    )
    mine = master[:, :ROW_NEW].astype(jnp.bfloat16).reshape(8, ROW_NEW * LANES)
    params = lax.all_to_all(
        jnp.broadcast_to(mine[None], (16, 8, ROW_NEW * LANES)), ("y", "x"), 0, 0, tiled=True
    ).reshape(128, ROW_NEW * LANES)

    near = jnp.where(own >= new_start, block, block_two).astype(jnp.float32)
    outs = pl.pallas_call(
        owner_kernel,
        out_shape=(jax.ShapeDtypeStruct((1, SLOT, LANES), jnp.float32),) * 3,
        in_specs=[smem, vmem, vmem, vmem],
        out_specs=(vmem, vmem, vmem),
        scratch_shapes=[pltpu.VMEM((3, 2 * SLOT, LANES), jnp.float32)],
        compiler_params=pltpu.CompilerParams(vmem_limit_bytes=24 * 1024 * 1024),
    )(place, near, block_one.astype(jnp.float32), grad)
    return (*outs, params)


def solution(mesh):
    fine = Mesh(mesh.devices.reshape(4, 4, 8), ("y", "x", "tensor"))
    parts = P(("y", "x", "tensor"), None, None)
    return jax.shard_map(
        on_device,
        mesh=fine,
        in_specs=(parts, parts, parts, parts, P(), P(), P()),
        out_specs=(parts, parts, parts, P(None, "tensor")),
        check_vma=False,
    )
```

```python
import functools
import jax
import jax.numpy as jnp
from jax import lax
from jax.experimental import pallas as pl
from jax.experimental.pallas import tpu as pltpu
from jax.sharding import Mesh, PartitionSpec as P

OLD_TP = 4
STEPS_DONE = 10
SLOT = 672
UNIT = 336
LANES = 128
ROW_OLD = 84
QUART = 21
QPAD = 24
ROW_NEW = 42
RPAD = 48

beta_first = 0.9
beta_second = 0.95
learn_rate = 0.1
decay_rate = 0.1
epsilon_add = 1e-08

SCALE_W = 2.0**13
SCALE_M = 2.0**15
SCALE_V = 2.0**15
SCALE_G = 2.0**13


def adam_update(master, moment, square, gradient):
    moment_new = beta_first * moment + (1.0 - beta_first) * gradient
    square_new = beta_second * square + (1.0 - beta_second) * gradient * gradient
    moment_hat = moment_new / (1.0 - beta_first**STEPS_DONE)
    square_hat = square_new / (1.0 - beta_second**STEPS_DONE)
    master_new = master - learn_rate * (
        moment_hat / (jnp.sqrt(square_hat) + epsilon_add) + decay_rate * master
    )
    return (master_new, moment_new, square_new)


def wrap(value):
    return jnp.where(value < 0, value + SLOT, value)


def pack_kernel(
    old_hbm, new_hbm, w_ref, m_ref, v_ref, g_ref, out_ref, gout_ref, info_ref,
    scratch, old_ref, new_ref, sems,
):
    tables = [
        pltpu.make_async_copy(old_hbm, old_ref, sems.at[4]),
        pltpu.make_async_copy(new_hbm, new_ref, sems.at[5]),
    ]
    for copy in tables:
        copy.start()
    copies = [
        pltpu.make_async_copy(ref.at[0], scratch.at[s, pl.ds(0, SLOT)], sems.at[s])
        for s, ref in enumerate((g_ref, w_ref, m_ref, v_ref))
    ]
    for copy in copies:
        copy.start()
    for copy in tables:
        copy.wait()
    dp = lax.axis_index("y") * 4 + lax.axis_index("x")
    tp = lax.axis_index("tensor")
    old_start = lax.rem(old_ref[1, dp * 8 + tp], SLOT)
    new_start = new_ref[1, dp * 8 + tp]
    new_place = lax.rem(new_start - dp * UNIT, SLOT)
    above = lax.rem(dp + 1, 16)
    info_ref[0] = jnp.full((8, LANES), new_start, jnp.int32)
    info_ref[1] = jnp.full((8, LANES), new_ref[1, above * 8 + tp], jnp.int32)
    for s, copy in enumerate(copies):
        copy.wait()
        scratch[s, pl.ds(SLOT, RPAD), :] = scratch[s, pl.ds(0, RPAD), :]
        if s == 0:
            for half in range(2):
                for t in range(8):
                    offset = wrap(half * UNIT + t * ROW_NEW - new_place)
                    gout_ref[half, t] = scratch[0, pl.ds(offset, RPAD), :] * SCALE_G
            continue
        scale = (SCALE_W, SCALE_M, SCALE_V)[s - 1]
        for hq in range(4):
            for t in range(8):
                offset = wrap(t * ROW_OLD + hq * QUART - old_start)
                piece = scratch[s, pl.ds(offset, QPAD), :]
                out_ref[hq * 8 + t, :, pl.ds((s - 1) * LANES, LANES)] = piece * scale


def owner_kernel(new_ref, ends_ref, mid_ref, g_ref, w_out, m_out, v_out, scratch):
    dp = lax.axis_index("y") * 4 + lax.axis_index("x")
    tp = lax.axis_index("tensor")
    new_place = lax.rem(new_ref[1, dp * 8 + tp] - dp * UNIT, SLOT)
    length = new_ref[2, dp * 8 + tp]
    for half, ref in enumerate((ends_ref, mid_ref)):
        for t in range(8):
            for s in range(3):
                piece = ref[t, pl.ds(0, ROW_NEW), pl.ds(s * LANES, LANES)]
                at = half * UNIT + t * ROW_NEW
                scratch[s, pl.ds(at, ROW_NEW), :] = piece
                scratch[s, pl.ds(at + SLOT, ROW_NEW), :] = piece
    step = 96
    for c in range(SLOT // step):
        at = new_place + c * step
        w = scratch[0, pl.ds(at, step), :] * (1.0 / SCALE_W)
        m = scratch[1, pl.ds(at, step), :] * (1.0 / SCALE_M)
        v = scratch[2, pl.ds(at, step), :] * (1.0 / SCALE_V)
        rows = pl.ds(c * step, step)
        slot = lax.broadcasted_iota(jnp.int32, (step, LANES), 0) + c * step
        inside = slot < length
        new = adam_update(w, m, v, g_ref[0, rows, :])
        for ref, value in zip((w_out, m_out, v_out), new):
            ref[0, rows, :] = jnp.where(inside, value, 0.0)


def one_hot_dot(chosen, source):
    picked = jnp.dot(
        chosen.astype(jnp.float32),
        source.astype(jnp.float32),
        precision=lax.Precision.HIGH,
        preferred_element_type=jnp.float32,
    )
    return picked.astype(jnp.float16)


def on_device(old_master, old_avg, old_sq, grad, old_table, new_table, head_order):
    y = lax.axis_index("y")
    x = lax.axis_index("x")
    t = lax.axis_index("tensor")
    dp = y * 4 + x
    f16 = jnp.float16

    vmem = pl.BlockSpec(memory_space=pltpu.VMEM)
    smem = pl.BlockSpec(memory_space=pltpu.SMEM)
    hbm = pl.BlockSpec(memory_space=pltpu.HBM)
    packed, grad_rows, info = pl.pallas_call(
        pack_kernel,
        out_shape=(
            pltpu.VMEM((32, QPAD, 3 * LANES), jnp.float32),
            pltpu.VMEM((2, 8, RPAD, LANES), jnp.float32),
            pltpu.VMEM((2, 8, LANES), jnp.int32),
        ),
        in_specs=[hbm] * 6,
        out_specs=(vmem, vmem, vmem),
        scratch_shapes=[
            pltpu.VMEM((4, SLOT + RPAD, LANES), jnp.float32),
            pltpu.SMEM((3, 128), jnp.int32),
            pltpu.SMEM((3, 128), jnp.int32),
            pltpu.SemaphoreType.DMA((6,)),
        ],
    )(old_table.T, new_table.T, old_master, old_avg, old_sq, grad)

    up = [(i, (i + 1) % 16) for i in range(16)]
    down = [(i, (i - 1) % 16) for i in range(16)]

    first = lax.all_to_all(packed.astype(f16), ("x", "tensor"), 0, 0, tiled=True)

    grad_rows, first = lax.optimization_barrier((grad_rows, first))
    grad_send = grad_rows.astype(f16)
    grad_first = lax.ppermute(grad_send[0], ("y", "x"), down)
    grad_last = lax.ppermute(grad_send[0], ("y", "x"), up)

    ranks = lax.dynamic_slice_in_dim(old_table, y * 32, 32, 0)
    begin = jnp.broadcast_to(ranks[:, 1:2], (32, QPAD)).reshape(1, 32 * QPAD)
    end = begin + jnp.broadcast_to(ranks[:, 2:3], (32, QPAD)).reshape(1, 32 * QPAD)
    row_id = lax.broadcasted_iota(jnp.int32, (16 * QPAD, 32 * QPAD), 0)
    col_id = lax.broadcasted_iota(jnp.int32, (16 * QPAD, 32 * QPAD), 1)
    j = row_id % QPAD
    flat = (((row_id // QPAD + 1) % 16) * 8 + t) * ROW_OLD + x * QUART + j
    chosen = (j == col_id % QPAD) & (j < QUART) & (flat >= begin) & (flat < end)
    chosen = lax.optimization_barrier(chosen.astype(jnp.bfloat16))
    rows = one_hot_dot(chosen, first.reshape(32 * QPAD, 3 * LANES))

    second = lax.all_to_all(
        rows.reshape(16, QPAD, 3 * LANES), ("y", "x"), 0, 0, tiled=True
    )
    order = head_order.reshape(8, 1, 14)
    comp = jnp.arange(3, dtype=jnp.int32).reshape(1, 3, 1)
    origin = (order // 7) * QPAD + (order % 7) * 3 + comp
    origin = jnp.pad(origin.reshape(8, ROW_NEW), ((0, 0), (0, RPAD - ROW_NEW)))
    origin = origin.reshape(8 * RPAD, 1)
    col_id = lax.broadcasted_iota(jnp.int32, (8 * RPAD, 16 * QPAD), 1)
    moved = lax.optimization_barrier((origin == col_id).astype(jnp.bfloat16))
    heads = one_hot_dot(moved, second.reshape(16 * QPAD, 3 * LANES))

    block = lax.all_to_all(heads.reshape(8, RPAD, 3 * LANES), "tensor", 0, 0, tiled=True)

    above = (dp + 1) % 16
    own = lax.broadcasted_iota(jnp.int32, (8, RPAD, LANES), 0) * ROW_NEW
    own = own + lax.broadcasted_iota(jnp.int32, (8, RPAD, LANES), 1)
    gradient = jnp.where(
        own >= info[1, 0] - above * UNIT,
        grad_first.astype(jnp.float32),
        jnp.where(
            own >= info[0, 0] - above * UNIT,
            grad_send[1].astype(jnp.float32),
            grad_last.astype(jnp.float32),
        ),
    ) * (1.0 / SCALE_G)
    wide = block.astype(jnp.float32)
    master, _, _ = adam_update(
        wide[:, :, :LANES] * (1.0 / SCALE_W),
        wide[:, :, LANES : 2 * LANES] * (1.0 / SCALE_M),
        wide[:, :, 2 * LANES :] * (1.0 / SCALE_V),
        gradient,
    )
    mine = master[:, :ROW_NEW].astype(jnp.bfloat16).reshape(8, ROW_NEW * LANES)
    mine = jnp.broadcast_to(mine[None], (16, 8, ROW_NEW * LANES))
    mine, block = lax.optimization_barrier((mine, block))
    spread = lax.all_to_all(mine, ("y", "x"), 0, 0, tiled=True)
    params = jnp.concatenate([spread[15:], spread[:15]]).reshape(128, ROW_NEW * LANES)

    block_near = lax.ppermute(block, ("y", "x"), up)
    block_far = lax.ppermute(block, ("y", "x"), down)
    own = jnp.concatenate([own] * 3, axis=2)
    near = own >= jnp.concatenate([info[0, 0]] * 3) - dp * UNIT
    ends = jnp.where(near, block_near, block_far).astype(jnp.float32)
    outs = pl.pallas_call(
        owner_kernel,
        out_shape=(jax.ShapeDtypeStruct((1, SLOT, LANES), jnp.float32),) * 3,
        in_specs=[smem, vmem, vmem, vmem],
        out_specs=(vmem, vmem, vmem),
        scratch_shapes=[pltpu.VMEM((3, 2 * SLOT, LANES), jnp.float32)],
        compiler_params=pltpu.CompilerParams(vmem_limit_bytes=24 * 1024 * 1024),
    )(new_table.T, ends, block.astype(jnp.float32), grad)
    return (*outs, params)


def solution(mesh):
    fine = Mesh(mesh.devices.reshape(4, 4, 8), ("y", "x", "tensor"))
    parts = P(("y", "x", "tensor"), None, None)
    return jax.shard_map(
        on_device,
        mesh=fine,
        in_specs=(parts, parts, parts, parts, P(), P(), P()),
        out_specs=(parts, parts, parts, P(None, "tensor")),
        check_vma=False,
    )
```

```python
import functools
import jax
import jax.numpy as jnp
from jax import lax
from jax.experimental import pallas as pl
from jax.experimental.pallas import tpu as pltpu
from jax.sharding import Mesh, PartitionSpec as P

OLD_TP = 4
STEPS_DONE = 10
SLOT = 672
UNIT = 336
LANES = 128
ROW_OLD = 84
QUART = 21
QPAD = 24
ROW_NEW = 42
RPAD = 48
PAIR = 88
HALF = ROW_NEW * LANES // 2
TURNS = (0, 1, 3, 2)

beta_first = 0.9
beta_second = 0.95
learn_rate = 0.1
decay_rate = 0.1
epsilon_add = 1e-08

SCALE_W = 2.0**13
SCALE_M = 2.0**15
SCALE_V = 2.0**15
SCALE_G = 2.0**13


def adam_update(master, moment, square, gradient):
    moment_new = beta_first * moment + (1.0 - beta_first) * gradient
    square_new = beta_second * square + (1.0 - beta_second) * gradient * gradient
    moment_hat = moment_new / (1.0 - beta_first**STEPS_DONE)
    square_hat = square_new / (1.0 - beta_second**STEPS_DONE)
    master_new = master - learn_rate * (
        moment_hat / (jnp.sqrt(square_hat) + epsilon_add) + decay_rate * master
    )
    return (master_new, moment_new, square_new)


def wrap(value):
    return jnp.where(value < 0, value + SLOT, value)


def pack_kernel(
    old_hbm, new_hbm, w_ref, m_ref, v_ref, g_ref, out_ref, gout_ref, info_ref,
    scratch, old_ref, new_ref, sems,
):
    tables = [
        pltpu.make_async_copy(old_hbm, old_ref, sems.at[4]),
        pltpu.make_async_copy(new_hbm, new_ref, sems.at[5]),
    ]
    for copy in tables:
        copy.start()
    copies = [
        pltpu.make_async_copy(ref.at[0], scratch.at[s, pl.ds(0, SLOT)], sems.at[s])
        for s, ref in enumerate((g_ref, w_ref, m_ref, v_ref))
    ]
    for copy in copies:
        copy.start()
    for copy in tables:
        copy.wait()
    dp = lax.axis_index("y") * 4 + lax.axis_index("x")
    tp = lax.axis_index("tensor")
    old_start = lax.rem(old_ref[1, dp * 8 + tp], SLOT)
    new_start = new_ref[1, dp * 8 + tp]
    new_place = lax.rem(new_start - dp * UNIT, SLOT)
    above = lax.rem(dp + 1, 16)
    info_ref[0] = jnp.full((8, LANES), new_ref[1, above * 8 + tp] - above * UNIT, jnp.int32)
    info_ref[1] = jnp.full((8, LANES), new_start - above * UNIT, jnp.int32)
    for s, copy in enumerate(copies):
        copy.wait()
        scratch[s, pl.ds(SLOT, RPAD), :] = scratch[s, pl.ds(0, RPAD), :]
        if s == 0:
            for half in range(2):
                for t in range(8):
                    offset = wrap(half * UNIT + t * ROW_NEW - new_place)
                    gout_ref[half, t] = scratch[0, pl.ds(offset, RPAD), :] * SCALE_G
            continue
        scale = (SCALE_W, SCALE_M, SCALE_V)[s - 1]
        for hq in range(4):
            for t in range(8):
                offset = wrap(t * ROW_OLD + hq * QUART - old_start)
                piece = scratch[s, pl.ds(offset, QPAD), :]
                out_ref[hq * 8 + t, :, pl.ds((s - 1) * LANES, LANES)] = piece * scale


def owner_kernel(new_ref, rows_ref, g_ref, w_out, m_out, v_out, scratch):
    dp = lax.axis_index("y") * 4 + lax.axis_index("x")
    tp = lax.axis_index("tensor")
    new_place = lax.rem(new_ref[1, dp * 8 + tp] - dp * UNIT, SLOT)
    length = new_ref[2, dp * 8 + tp]
    for half in range(2):
        for t in range(8):
            for s in range(3):
                piece = rows_ref[t, pl.ds((1 - half) * ROW_NEW, ROW_NEW), pl.ds(s * LANES, LANES)]
                at = half * UNIT + t * ROW_NEW
                scratch[s, pl.ds(at, ROW_NEW), :] = piece
                scratch[s, pl.ds(at + SLOT, ROW_NEW), :] = piece
    step = 96
    for c in range(SLOT // step):
        at = new_place + c * step
        w = scratch[0, pl.ds(at, step), :] * (1.0 / SCALE_W)
        m = scratch[1, pl.ds(at, step), :] * (1.0 / SCALE_M)
        v = scratch[2, pl.ds(at, step), :] * (1.0 / SCALE_V)
        rows = pl.ds(c * step, step)
        slot = lax.broadcasted_iota(jnp.int32, (step, LANES), 0) + c * step
        inside = slot < length
        new = adam_update(w, m, v, g_ref[0, rows, :])
        for ref, value in zip((w_out, m_out, v_out), new):
            ref[0, rows, :] = jnp.where(inside, value, 0.0)


def place_kernel(*refs):
    pieces, out_ref = refs[:8], refs[8]
    y, x = lax.axis_index("y"), lax.axis_index("x")
    for half in range(2):
        for k in range(4):
            for l in range(4):
                dy, dx = (k, l) if half == 0 else (l, k)
                from_y = lax.rem(y + 4 - TURNS[dy], 4)
                from_x = lax.rem(x + 4 - TURNS[dx], 4)
                block = lax.rem(from_y * 4 + from_x + 1, 16)
                out_ref[block, :, pl.ds(half * HALF, HALF)] = pieces[half * 4 + k][l]


def one_hot_dot(chosen, source):
    picked = jnp.dot(
        chosen.astype(jnp.float32),
        source.astype(jnp.float32),
        precision=lax.Precision.HIGH,
        preferred_element_type=jnp.float32,
    )
    return picked.astype(jnp.float16)


def on_device(old_master, old_avg, old_sq, grad, old_table, new_table, head_order):
    y = lax.axis_index("y")
    x = lax.axis_index("x")
    t = lax.axis_index("tensor")
    dp = y * 4 + x
    f16 = jnp.float16

    vmem = pl.BlockSpec(memory_space=pltpu.VMEM)
    smem = pl.BlockSpec(memory_space=pltpu.SMEM)
    hbm = pl.BlockSpec(memory_space=pltpu.HBM)
    packed, grad_rows, info = pl.pallas_call(
        pack_kernel,
        out_shape=(
            pltpu.VMEM((32, QPAD, 3 * LANES), jnp.float32),
            pltpu.VMEM((2, 8, RPAD, LANES), jnp.float32),
            pltpu.VMEM((2, 8, LANES), jnp.int32),
        ),
        in_specs=[hbm] * 6,
        out_specs=(vmem, vmem, vmem),
        scratch_shapes=[
            pltpu.VMEM((4, SLOT + RPAD, LANES), jnp.float32),
            pltpu.SMEM((3, 128), jnp.int32),
            pltpu.SMEM((3, 128), jnp.int32),
            pltpu.SemaphoreType.DMA((6,)),
        ],
    )(old_table.T, new_table.T, old_master, old_avg, old_sq, grad)

    up = [(i, (i + 1) % 16) for i in range(16)]
    down = [(i, (i - 1) % 16) for i in range(16)]

    first = lax.all_to_all(packed.astype(f16), ("x", "tensor"), 0, 0, tiled=True)

    grad_rows, first = lax.optimization_barrier((grad_rows, first))
    grad_send = grad_rows.astype(f16)
    grad_first = lax.ppermute(grad_send[0], ("y", "x"), down)
    grad_last = lax.ppermute(grad_send[0], ("y", "x"), up)

    ranks = lax.dynamic_slice_in_dim(old_table, y * 32, 32, 0)
    begin = jnp.broadcast_to(ranks[:, 1:2], (32, QPAD)).reshape(1, 32 * QPAD)
    end = begin + jnp.broadcast_to(ranks[:, 2:3], (32, QPAD)).reshape(1, 32 * QPAD)
    heads_here = y * 28 + x * 7 + jnp.arange(7, dtype=jnp.int32)
    at_head = head_order[None, :] == heads_here[:, None]
    position = jnp.sum(jnp.where(at_head, jnp.arange(112, dtype=jnp.int32)[None, :], 0), axis=1)
    rank_new, j_new = position // 14, position % 14
    starts = new_table[:, 1].reshape(16, 1, 8)
    at_rank = rank_new[None, :, None] == jnp.arange(8, dtype=jnp.int32)[None, None, :]
    edge = jnp.sum(jnp.where(at_rank, starts, 0), axis=2)
    e = jnp.arange(16, dtype=jnp.int32)
    edge = edge - e[:, None] * UNIT - t * ROW_NEW - j_new[None, :]
    near = 14 * jnp.arange(3, dtype=jnp.int32)[None, None, :] >= edge[:, :, None]
    near = jnp.pad(near.reshape(16, QUART), ((0, 0), (0, QPAD - QUART)))
    block_end = jnp.where(near, e[:, None], (e[:, None] + 2) % 16)
    block_own = jnp.broadcast_to((e[:, None] + 1) % 16, (16, QPAD))
    source = jnp.stack([block_own, block_end], axis=1)
    j = jnp.arange(QPAD, dtype=jnp.int32)[None, None, :]
    flat = (source * 8 + t) * ROW_OLD + x * QUART + j
    flat = jnp.where(j < QUART, flat, -1).reshape(32 * QPAD, 1)
    row_id = lax.broadcasted_iota(jnp.int32, (32 * QPAD, 32 * QPAD), 0)
    col_id = lax.broadcasted_iota(jnp.int32, (32 * QPAD, 32 * QPAD), 1)
    chosen = (row_id % QPAD == col_id % QPAD) & (flat >= begin) & (flat < end)
    chosen = lax.optimization_barrier(chosen.astype(jnp.bfloat16))
    rows = one_hot_dot(chosen, first.reshape(32 * QPAD, 3 * LANES))

    second = lax.all_to_all(
        rows.reshape(16, 2 * QPAD, 3 * LANES), ("y", "x"), 0, 0, tiled=True
    )
    order = head_order.reshape(8, 1, 1, 14)
    kind = jnp.arange(2, dtype=jnp.int32).reshape(1, 2, 1, 1)
    comp = jnp.arange(3, dtype=jnp.int32).reshape(1, 1, 3, 1)
    origin = ((order // 7) * 2 + kind) * QPAD + (order % 7) * 3 + comp
    origin = jnp.pad(origin.reshape(8, 2 * ROW_NEW), ((0, 0), (0, PAIR - 2 * ROW_NEW)))
    origin = origin.reshape(8 * PAIR, 1)
    col_id = lax.broadcasted_iota(jnp.int32, (8 * PAIR, 32 * QPAD), 1)
    moved = lax.optimization_barrier((origin == col_id).astype(jnp.bfloat16))
    heads = one_hot_dot(moved, second.reshape(32 * QPAD, 3 * LANES))

    block = lax.all_to_all(heads.reshape(8, PAIR, 3 * LANES), "tensor", 0, 0, tiled=True)

    own = lax.broadcasted_iota(jnp.int32, (8, RPAD, LANES), 0) * ROW_NEW
    own = own + lax.broadcasted_iota(jnp.int32, (8, RPAD, LANES), 1)
    gradient = jnp.where(
        own >= info[0, 0],
        grad_first.astype(jnp.float32),
        jnp.where(
            own >= info[1, 0],
            grad_send[1].astype(jnp.float32),
            grad_last.astype(jnp.float32),
        ),
    ) * (1.0 / SCALE_G)
    wide = block[:, :RPAD].astype(jnp.float32)
    master, _, _ = adam_update(
        wide[:, :, :LANES] * (1.0 / SCALE_W),
        wide[:, :, LANES : 2 * LANES] * (1.0 / SCALE_M),
        wide[:, :, 2 * LANES :] * (1.0 / SCALE_V),
        gradient,
    )
    mine = master[:, :ROW_NEW].astype(jnp.bfloat16).reshape(8, ROW_NEW * LANES)

    def turn(value, axis):
        return [value] + [
            lax.ppermute(value, axis, [(i, (i + by) % 4) for i in range(4)])
            for by in TURNS[1:]
        ]

    by_x = jnp.stack(turn(mine[:, :HALF], "x"))
    by_y = jnp.stack(turn(mine[:, HALF:], "y"))
    pieces = turn(by_x, "y") + turn(by_y, "x")
    params = pl.pallas_call(
        place_kernel,
        out_shape=jax.ShapeDtypeStruct((16, 8, ROW_NEW * LANES), jnp.bfloat16),
        in_specs=[vmem] * 8,
        out_specs=vmem,
        compiler_params=pltpu.CompilerParams(vmem_limit_bytes=16 * 1024 * 1024),
    )(*pieces).reshape(128, ROW_NEW * LANES)

    outs = pl.pallas_call(
        owner_kernel,
        out_shape=(jax.ShapeDtypeStruct((1, SLOT, LANES), jnp.float32),) * 3,
        in_specs=[smem, vmem, vmem],
        out_specs=(vmem, vmem, vmem),
        scratch_shapes=[pltpu.VMEM((3, 2 * SLOT, LANES), jnp.float32)],
        compiler_params=pltpu.CompilerParams(vmem_limit_bytes=24 * 1024 * 1024),
    )(new_table.T, block.astype(jnp.float32), grad)
    return (*outs, params)


def solution(mesh):
    fine = Mesh(mesh.devices.reshape(4, 4, 8), ("y", "x", "tensor"))
    parts = P(("y", "x", "tensor"), None, None)
    return jax.shard_map(
        on_device,
        mesh=fine,
        in_specs=(parts, parts, parts, parts, P(), P(), P()),
        out_specs=(parts, parts, parts, P(None, "tensor")),
        check_vma=False,
    )
```

```python
import functools
import jax
import jax.numpy as jnp
from jax import lax
from jax.experimental import pallas as pl
from jax.experimental.pallas import tpu as pltpu
from jax.sharding import Mesh, PartitionSpec as P

OLD_TP = 4
STEPS_DONE = 10
SLOT = 672
UNIT = 336
LANES = 128
ROW_OLD = 84
QUART = 21
QPAD = 24
ROW_NEW = 42
RPAD = 48
PAIR = 88
HALF = ROW_NEW * LANES // 2
TURNS = (0, 2, 1, 3)

beta_first = 0.9
beta_second = 0.95
learn_rate = 0.1
decay_rate = 0.1
epsilon_add = 1e-08

SCALE_W = 2.0**13
SCALE_M = 2.0**15
SCALE_V = 2.0**15
SCALE_G = 2.0**13


def adam_update(master, moment, square, gradient):
    moment_new = beta_first * moment + (1.0 - beta_first) * gradient
    square_new = beta_second * square + (1.0 - beta_second) * gradient * gradient
    moment_hat = moment_new / (1.0 - beta_first**STEPS_DONE)
    square_hat = square_new / (1.0 - beta_second**STEPS_DONE)
    master_new = master - learn_rate * (
        moment_hat / (jnp.sqrt(square_hat) + epsilon_add) + decay_rate * master
    )
    return (master_new, moment_new, square_new)


def wrap(value):
    return jnp.where(value < 0, value + SLOT, value)


def pack_kernel(
    old_hbm, new_hbm, w_ref, m_ref, v_ref, g_ref, out_ref, gout_ref, info_ref,
    scratch, old_ref, new_ref, sems,
):
    tables = [
        pltpu.make_async_copy(old_hbm, old_ref, sems.at[4]),
        pltpu.make_async_copy(new_hbm, new_ref, sems.at[5]),
    ]
    for copy in tables:
        copy.start()
    copies = [
        pltpu.make_async_copy(ref.at[0], scratch.at[s, pl.ds(0, SLOT)], sems.at[s])
        for s, ref in enumerate((g_ref, w_ref, m_ref, v_ref))
    ]
    for copy in copies:
        copy.start()
    for copy in tables:
        copy.wait()
    dp = lax.axis_index("y") * 4 + lax.axis_index("x")
    tp = lax.axis_index("tensor")
    old_start = lax.rem(old_ref[1, dp * 8 + tp], SLOT)
    new_start = new_ref[1, dp * 8 + tp]
    new_place = lax.rem(new_start - dp * UNIT, SLOT)
    above = lax.rem(dp + 1, 16)
    info_ref[0] = jnp.full((8, LANES), new_ref[1, above * 8 + tp] - above * UNIT, jnp.int32)
    info_ref[1] = jnp.full((8, LANES), new_start - above * UNIT, jnp.int32)
    for s, copy in enumerate(copies):
        copy.wait()
        scratch[s, pl.ds(SLOT, RPAD), :] = scratch[s, pl.ds(0, RPAD), :]
        if s == 0:
            for half in range(2):
                for t in range(8):
                    offset = wrap(half * UNIT + t * ROW_NEW - new_place)
                    gout_ref[half, t] = scratch[0, pl.ds(offset, RPAD), :] * SCALE_G
            continue
        scale = (SCALE_W, SCALE_M, SCALE_V)[s - 1]
        for hq in range(4):
            for t in range(8):
                offset = wrap(t * ROW_OLD + hq * QUART - old_start)
                piece = scratch[s, pl.ds(offset, QPAD), :]
                out_ref[hq * 8 + t, :, pl.ds((s - 1) * LANES, LANES)] = piece * scale


def owner_kernel(new_ref, rows_ref, g_ref, w_out, m_out, v_out, scratch):
    dp = lax.axis_index("y") * 4 + lax.axis_index("x")
    tp = lax.axis_index("tensor")
    new_place = lax.rem(new_ref[1, dp * 8 + tp] - dp * UNIT, SLOT)
    length = new_ref[2, dp * 8 + tp]
    for half in range(2):
        for t in range(8):
            for s in range(3):
                piece = rows_ref[t, pl.ds((1 - half) * ROW_NEW, ROW_NEW), pl.ds(s * LANES, LANES)]
                at = half * UNIT + t * ROW_NEW
                scratch[s, pl.ds(at, ROW_NEW), :] = piece
                scratch[s, pl.ds(at + SLOT, ROW_NEW), :] = piece
    step = 96
    for c in range(SLOT // step):
        at = new_place + c * step
        w = scratch[0, pl.ds(at, step), :] * (1.0 / SCALE_W)
        m = scratch[1, pl.ds(at, step), :] * (1.0 / SCALE_M)
        v = scratch[2, pl.ds(at, step), :] * (1.0 / SCALE_V)
        rows = pl.ds(c * step, step)
        slot = lax.broadcasted_iota(jnp.int32, (step, LANES), 0) + c * step
        inside = slot < length
        new = adam_update(w, m, v, g_ref[0, rows, :])
        for ref, value in zip((w_out, m_out, v_out), new):
            ref[0, rows, :] = jnp.where(inside, value, 0.0)


def place_kernel(*refs):
    pieces, out_ref = refs[:8], refs[8]
    y, x = lax.axis_index("y"), lax.axis_index("x")
    for half in range(2):
        for k in range(4):
            for l in range(4):
                dy, dx = (k, l) if half == 0 else (l, k)
                from_y = lax.rem(y + 4 - TURNS[dy], 4)
                from_x = lax.rem(x + 4 - TURNS[dx], 4)
                block = lax.rem(from_y * 4 + from_x + 1, 16)
                out_ref[block, :, pl.ds(half * HALF, HALF)] = pieces[half * 4 + k][l]


def one_hot_dot(chosen, source):
    picked = jnp.dot(
        chosen.astype(jnp.float32),
        source.astype(jnp.float32),
        precision=lax.Precision.HIGH,
        preferred_element_type=jnp.float32,
    )
    return picked.astype(jnp.float16)


def on_device(old_master, old_avg, old_sq, grad, old_table, new_table, head_order):
    y = lax.axis_index("y")
    x = lax.axis_index("x")
    t = lax.axis_index("tensor")
    dp = y * 4 + x
    f16 = jnp.float16

    vmem = pl.BlockSpec(memory_space=pltpu.VMEM)
    smem = pl.BlockSpec(memory_space=pltpu.SMEM)
    hbm = pl.BlockSpec(memory_space=pltpu.HBM)
    packed, grad_rows, info = pl.pallas_call(
        pack_kernel,
        out_shape=(
            pltpu.VMEM((32, QPAD, 3 * LANES), jnp.float32),
            pltpu.VMEM((2, 8, RPAD, LANES), jnp.float32),
            pltpu.VMEM((2, 8, LANES), jnp.int32),
        ),
        in_specs=[hbm] * 6,
        out_specs=(vmem, vmem, vmem),
        scratch_shapes=[
            pltpu.VMEM((4, SLOT + RPAD, LANES), jnp.float32),
            pltpu.SMEM((3, 128), jnp.int32),
            pltpu.SMEM((3, 128), jnp.int32),
            pltpu.SemaphoreType.DMA((6,)),
        ],
    )(old_table.T, new_table.T, old_master, old_avg, old_sq, grad)

    up = [(i, (i + 1) % 16) for i in range(16)]
    down = [(i, (i - 1) % 16) for i in range(16)]

    first = lax.all_to_all(packed.astype(f16), ("x", "tensor"), 0, 0, tiled=True)

    grad_rows, first = lax.optimization_barrier((grad_rows, first))
    grad_send = grad_rows.astype(f16)
    grad_first = lax.ppermute(grad_send[0], ("y", "x"), down)
    grad_last = lax.ppermute(grad_send[0], ("y", "x"), up)

    ranks = lax.dynamic_slice_in_dim(old_table, y * 32, 32, 0)
    begin = jnp.broadcast_to(ranks[:, 1:2], (32, QPAD)).reshape(1, 32 * QPAD)
    end = begin + jnp.broadcast_to(ranks[:, 2:3], (32, QPAD)).reshape(1, 32 * QPAD)
    heads_here = y * 28 + x * 7 + jnp.arange(7, dtype=jnp.int32)
    at_head = head_order[None, :] == heads_here[:, None]
    position = jnp.sum(jnp.where(at_head, jnp.arange(112, dtype=jnp.int32)[None, :], 0), axis=1)
    rank_new, j_new = position // 14, position % 14
    starts = new_table[:, 1].reshape(16, 1, 8)
    at_rank = rank_new[None, :, None] == jnp.arange(8, dtype=jnp.int32)[None, None, :]
    edge = jnp.sum(jnp.where(at_rank, starts, 0), axis=2)
    e = jnp.arange(16, dtype=jnp.int32)
    edge = edge - e[:, None] * UNIT - t * ROW_NEW - j_new[None, :]
    near = 14 * jnp.arange(3, dtype=jnp.int32)[None, None, :] >= edge[:, :, None]
    near = jnp.pad(near.reshape(16, QUART), ((0, 0), (0, QPAD - QUART)))
    block_end = jnp.where(near, e[:, None], (e[:, None] + 2) % 16)
    block_own = jnp.broadcast_to((e[:, None] + 1) % 16, (16, QPAD))
    source = jnp.stack([block_own, block_end], axis=1)
    j = jnp.arange(QPAD, dtype=jnp.int32)[None, None, :]
    flat = (source * 8 + t) * ROW_OLD + x * QUART + j
    flat = jnp.where(j < QUART, flat, -1).reshape(32 * QPAD, 1)
    row_id = lax.broadcasted_iota(jnp.int32, (32 * QPAD, 32 * QPAD), 0)
    col_id = lax.broadcasted_iota(jnp.int32, (32 * QPAD, 32 * QPAD), 1)
    chosen = (row_id % QPAD == col_id % QPAD) & (flat >= begin) & (flat < end)
    chosen = lax.optimization_barrier(chosen.astype(jnp.bfloat16))
    rows = one_hot_dot(chosen, first.reshape(32 * QPAD, 3 * LANES))

    second = lax.all_to_all(
        rows.reshape(16, 2 * QPAD, 3 * LANES), ("y", "x"), 0, 0, tiled=True
    )
    order = head_order.reshape(8, 1, 1, 14)
    kind = jnp.arange(2, dtype=jnp.int32).reshape(1, 2, 1, 1)
    comp = jnp.arange(3, dtype=jnp.int32).reshape(1, 1, 3, 1)
    origin = ((order // 7) * 2 + kind) * QPAD + (order % 7) * 3 + comp
    origin = jnp.pad(origin.reshape(8, 2 * ROW_NEW), ((0, 0), (0, PAIR - 2 * ROW_NEW)))
    origin = origin.reshape(8 * PAIR, 1)
    col_id = lax.broadcasted_iota(jnp.int32, (8 * PAIR, 32 * QPAD), 1)
    moved = lax.optimization_barrier((origin == col_id).astype(jnp.bfloat16))
    heads = one_hot_dot(moved, second.reshape(32 * QPAD, 3 * LANES))

    block = lax.all_to_all(heads.reshape(8, PAIR, 3 * LANES), "tensor", 0, 0, tiled=True)

    own = lax.broadcasted_iota(jnp.int32, (8, RPAD, LANES), 0) * ROW_NEW
    own = own + lax.broadcasted_iota(jnp.int32, (8, RPAD, LANES), 1)
    gradient = jnp.where(
        own >= info[0, 0],
        grad_first.astype(jnp.float32),
        jnp.where(
            own >= info[1, 0],
            grad_send[1].astype(jnp.float32),
            grad_last.astype(jnp.float32),
        ),
    ) * (1.0 / SCALE_G)
    wide = block[:, :RPAD].astype(jnp.float32)
    master, _, _ = adam_update(
        wide[:, :, :LANES] * (1.0 / SCALE_W),
        wide[:, :, LANES : 2 * LANES] * (1.0 / SCALE_M),
        wide[:, :, 2 * LANES :] * (1.0 / SCALE_V),
        gradient,
    )
    mine = master[:, :ROW_NEW].astype(jnp.bfloat16).reshape(8, ROW_NEW * LANES)

    def turn(value, axis):
        return [value] + [
            lax.ppermute(value, axis, [(i, (i + by) % 4) for i in range(4)])
            for by in TURNS[1:]
        ]

    by_x = jnp.stack(turn(mine[:, :HALF], "x"))
    by_y = jnp.stack(turn(mine[:, HALF:], "y"))
    pieces = turn(by_x, "y") + turn(by_y, "x")
    params = pl.pallas_call(
        place_kernel,
        out_shape=jax.ShapeDtypeStruct((16, 8, ROW_NEW * LANES), jnp.bfloat16),
        in_specs=[vmem] * 8,
        out_specs=vmem,
        compiler_params=pltpu.CompilerParams(vmem_limit_bytes=16 * 1024 * 1024),
    )(*pieces).reshape(128, ROW_NEW * LANES)

    outs = pl.pallas_call(
        owner_kernel,
        out_shape=(jax.ShapeDtypeStruct((1, SLOT, LANES), jnp.float32),) * 3,
        in_specs=[smem, vmem, vmem],
        out_specs=(vmem, vmem, vmem),
        scratch_shapes=[pltpu.VMEM((3, 2 * SLOT, LANES), jnp.float32)],
        compiler_params=pltpu.CompilerParams(vmem_limit_bytes=24 * 1024 * 1024),
    )(new_table.T, block.astype(jnp.float32), grad)
    return (*outs, params)


def solution(mesh):
    fine = Mesh(mesh.devices.reshape(4, 4, 8), ("y", "x", "tensor"))
    parts = P(("y", "x", "tensor"), None, None)
    return jax.shard_map(
        on_device,
        mesh=fine,
        in_specs=(parts, parts, parts, parts, P(), P(), P()),
        out_specs=(parts, parts, parts, P(None, "tensor")),
        check_vma=False,
    )
```

```python
import functools
import jax
import jax.numpy as jnp
from jax import lax
from jax.experimental import pallas as pl
from jax.experimental.pallas import tpu as pltpu
from jax.sharding import Mesh, PartitionSpec as P

OLD_TP = 4
STEPS_DONE = 10
SLOT = 672
UNIT = 336
LANES = 128
ROW_OLD = 84
QUART = 21
QPAD = 24
ROW_NEW = 42
RPAD = 48
PAIR = 88
TURNS = (0, 2, 1, 3)

beta_first = 0.9
beta_second = 0.95
learn_rate = 0.1
decay_rate = 0.1
epsilon_add = 1e-08

SCALE_W = 2.0**13
SCALE_M = 2.0**15
SCALE_V = 2.0**15
SCALE_G = 2.0**13


def adam_update(master, moment, square, gradient):
    moment_new = beta_first * moment + (1.0 - beta_first) * gradient
    square_new = beta_second * square + (1.0 - beta_second) * gradient * gradient
    moment_hat = moment_new / (1.0 - beta_first**STEPS_DONE)
    square_hat = square_new / (1.0 - beta_second**STEPS_DONE)
    master_new = master - learn_rate * (
        moment_hat / (jnp.sqrt(square_hat) + epsilon_add) + decay_rate * master
    )
    return (master_new, moment_new, square_new)


def wrap(value):
    return jnp.where(value < 0, value + SLOT, value)


def pack_kernel(
    old_hbm, new_hbm, w_ref, m_ref, v_ref, g_ref, out_ref, gout_ref, info_ref,
    scratch, old_ref, new_ref, sems,
):
    tables = [
        pltpu.make_async_copy(old_hbm, old_ref, sems.at[4]),
        pltpu.make_async_copy(new_hbm, new_ref, sems.at[5]),
    ]
    for copy in tables:
        copy.start()
    copies = [
        pltpu.make_async_copy(ref.at[0], scratch.at[s, pl.ds(0, SLOT)], sems.at[s])
        for s, ref in enumerate((g_ref, w_ref, m_ref, v_ref))
    ]
    for copy in copies:
        copy.start()
    for copy in tables:
        copy.wait()
    dp = lax.axis_index("y") * 4 + lax.axis_index("x")
    tp = lax.axis_index("z") * 2 + lax.axis_index("c")
    old_start = lax.rem(old_ref[1, dp * 8 + tp], SLOT)
    new_start = new_ref[1, dp * 8 + tp]
    new_place = lax.rem(new_start - dp * UNIT, SLOT)
    above = lax.rem(dp + 1, 16)
    info_ref[0] = jnp.full((8, LANES), new_ref[1, above * 8 + tp] - above * UNIT, jnp.int32)
    info_ref[1] = jnp.full((8, LANES), new_start - above * UNIT, jnp.int32)
    for s, copy in enumerate(copies):
        copy.wait()
        scratch[s, pl.ds(SLOT, RPAD), :] = scratch[s, pl.ds(0, RPAD), :]
        if s == 0:
            for half in range(2):
                for t in range(8):
                    offset = wrap(half * UNIT + t * ROW_NEW - new_place)
                    gout_ref[half, t] = scratch[0, pl.ds(offset, RPAD), :] * SCALE_G
            continue
        scale = (SCALE_W, SCALE_M, SCALE_V)[s - 1]
        for hq in range(4):
            for t in range(8):
                offset = wrap(t * ROW_OLD + hq * QUART - old_start)
                piece = scratch[s, pl.ds(offset, QPAD), :]
                out_ref[hq * 8 + t, :, pl.ds((s - 1) * LANES, LANES)] = piece * scale


def owner_kernel(new_ref, rows_ref, g_ref, w_out, m_out, v_out, scratch):
    dp = lax.axis_index("y") * 4 + lax.axis_index("x")
    tp = lax.axis_index("z") * 2 + lax.axis_index("c")
    new_place = lax.rem(new_ref[1, dp * 8 + tp] - dp * UNIT, SLOT)
    length = new_ref[2, dp * 8 + tp]
    for half in range(2):
        for t in range(8):
            for s in range(3):
                piece = rows_ref[t, pl.ds((1 - half) * ROW_NEW, ROW_NEW), pl.ds(s * LANES, LANES)]
                at = half * UNIT + t * ROW_NEW
                scratch[s, pl.ds(at, ROW_NEW), :] = piece
                scratch[s, pl.ds(at + SLOT, ROW_NEW), :] = piece
    step = 96
    for c in range(SLOT // step):
        at = new_place + c * step
        w = scratch[0, pl.ds(at, step), :] * (1.0 / SCALE_W)
        m = scratch[1, pl.ds(at, step), :] * (1.0 / SCALE_M)
        v = scratch[2, pl.ds(at, step), :] * (1.0 / SCALE_V)
        rows = pl.ds(c * step, step)
        slot = lax.broadcasted_iota(jnp.int32, (step, LANES), 0) + c * step
        inside = slot < length
        new = adam_update(w, m, v, g_ref[0, rows, :])
        for ref, value in zip((w_out, m_out, v_out), new):
            ref[0, rows, :] = jnp.where(inside, value, 0.0)


def place_kernel(*refs):
    held, out_ref = refs[:4], refs[4]
    y, x = lax.axis_index("y"), lax.axis_index("x")
    x_first = lax.axis_index("c") == 0
    for k in range(4):
        for l in range(4):
            dy = jnp.where(x_first, TURNS[k], TURNS[l])
            dx = jnp.where(x_first, TURNS[l], TURNS[k])
            block = lax.rem(lax.rem(y + 4 - dy, 4) * 4 + lax.rem(x + 4 - dx, 4) + 1, 16)
            out_ref[block] = held[k][l]


def one_hot_dot(chosen, source):
    picked = jnp.dot(
        chosen.astype(jnp.float32),
        source.astype(jnp.float32),
        precision=lax.Precision.HIGH,
        preferred_element_type=jnp.float32,
    )
    return picked.astype(jnp.float16)


def on_device(old_master, old_avg, old_sq, grad, old_table, new_table, head_order):
    y = lax.axis_index("y")
    x = lax.axis_index("x")
    core = lax.axis_index("c")
    t = lax.axis_index("z") * 2 + core
    dp = y * 4 + x
    f16 = jnp.float16

    vmem = pl.BlockSpec(memory_space=pltpu.VMEM)
    smem = pl.BlockSpec(memory_space=pltpu.SMEM)
    hbm = pl.BlockSpec(memory_space=pltpu.HBM)
    packed, grad_rows, info = pl.pallas_call(
        pack_kernel,
        out_shape=(
            pltpu.VMEM((32, QPAD, 3 * LANES), jnp.float32),
            pltpu.VMEM((2, 8, RPAD, LANES), jnp.float32),
            pltpu.VMEM((2, 8, LANES), jnp.int32),
        ),
        in_specs=[hbm] * 6,
        out_specs=(vmem, vmem, vmem),
        scratch_shapes=[
            pltpu.VMEM((4, SLOT + RPAD, LANES), jnp.float32),
            pltpu.SMEM((3, 128), jnp.int32),
            pltpu.SMEM((3, 128), jnp.int32),
            pltpu.SemaphoreType.DMA((6,)),
        ],
    )(old_table.T, new_table.T, old_master, old_avg, old_sq, grad)

    up = [(i, (i + 1) % 16) for i in range(16)]
    down = [(i, (i - 1) % 16) for i in range(16)]

    first = lax.all_to_all(packed.astype(f16), ("x", "z", "c"), 0, 0, tiled=True)

    grad_rows, first = lax.optimization_barrier((grad_rows, first))
    grad_send = grad_rows.astype(f16)
    grad_first = lax.ppermute(grad_send[0], ("y", "x"), down)
    grad_last = lax.ppermute(grad_send[0], ("y", "x"), up)

    ranks = lax.dynamic_slice_in_dim(old_table, y * 32, 32, 0)
    begin = jnp.broadcast_to(ranks[:, 1:2], (32, QPAD)).reshape(1, 32 * QPAD)
    end = begin + jnp.broadcast_to(ranks[:, 2:3], (32, QPAD)).reshape(1, 32 * QPAD)
    heads_here = y * 28 + x * 7 + jnp.arange(7, dtype=jnp.int32)
    at_head = head_order[None, :] == heads_here[:, None]
    position = jnp.sum(jnp.where(at_head, jnp.arange(112, dtype=jnp.int32)[None, :], 0), axis=1)
    rank_new, j_new = position // 14, position % 14
    starts = new_table[:, 1].reshape(16, 1, 8)
    at_rank = rank_new[None, :, None] == jnp.arange(8, dtype=jnp.int32)[None, None, :]
    edge = jnp.sum(jnp.where(at_rank, starts, 0), axis=2)
    e = jnp.arange(16, dtype=jnp.int32)
    edge = edge - e[:, None] * UNIT - t * ROW_NEW - j_new[None, :]
    near = 14 * jnp.arange(3, dtype=jnp.int32)[None, None, :] >= edge[:, :, None]
    near = jnp.pad(near.reshape(16, QUART), ((0, 0), (0, QPAD - QUART)))
    block_end = jnp.where(near, e[:, None], (e[:, None] + 2) % 16)
    block_own = jnp.broadcast_to((e[:, None] + 1) % 16, (16, QPAD))
    source = jnp.stack([block_own, block_end], axis=1)
    j = jnp.arange(QPAD, dtype=jnp.int32)[None, None, :]
    flat = (source * 8 + t) * ROW_OLD + x * QUART + j
    flat = jnp.where(j < QUART, flat, -1).reshape(32 * QPAD, 1)
    row_id = lax.broadcasted_iota(jnp.int32, (32 * QPAD, 32 * QPAD), 0)
    col_id = lax.broadcasted_iota(jnp.int32, (32 * QPAD, 32 * QPAD), 1)
    chosen = (row_id % QPAD == col_id % QPAD) & (flat >= begin) & (flat < end)
    chosen = lax.optimization_barrier(chosen.astype(jnp.bfloat16))
    rows = one_hot_dot(chosen, first.reshape(32 * QPAD, 3 * LANES))

    second = lax.all_to_all(
        rows.reshape(16, 2 * QPAD, 3 * LANES), ("y", "x"), 0, 0, tiled=True
    )
    order = head_order.reshape(8, 1, 1, 14)
    kind = jnp.arange(2, dtype=jnp.int32).reshape(1, 2, 1, 1)
    comp = jnp.arange(3, dtype=jnp.int32).reshape(1, 1, 3, 1)
    origin = ((order // 7) * 2 + kind) * QPAD + (order % 7) * 3 + comp
    origin = jnp.pad(origin.reshape(8, 2 * ROW_NEW), ((0, 0), (0, PAIR - 2 * ROW_NEW)))
    origin = origin.reshape(8 * PAIR, 1)
    col_id = lax.broadcasted_iota(jnp.int32, (8 * PAIR, 32 * QPAD), 1)
    moved = lax.optimization_barrier((origin == col_id).astype(jnp.bfloat16))
    heads = one_hot_dot(moved, second.reshape(32 * QPAD, 3 * LANES))

    block = lax.all_to_all(heads.reshape(8, PAIR, 3 * LANES), ("z", "c"), 0, 0, tiled=True)

    own = lax.broadcasted_iota(jnp.int32, (8, RPAD, LANES), 0) * ROW_NEW
    own = own + lax.broadcasted_iota(jnp.int32, (8, RPAD, LANES), 1)
    gradient = jnp.where(
        own >= info[0, 0],
        grad_first.astype(jnp.float32),
        jnp.where(
            own >= info[1, 0],
            grad_send[1].astype(jnp.float32),
            grad_last.astype(jnp.float32),
        ),
    ) * (1.0 / SCALE_G)
    wide = block[:, :RPAD].astype(jnp.float32)
    master, _, _ = adam_update(
        wide[:, :, :LANES] * (1.0 / SCALE_W),
        wide[:, :, LANES : 2 * LANES] * (1.0 / SCALE_M),
        wide[:, :, 2 * LANES :] * (1.0 / SCALE_V),
        gradient,
    )
    mine = master[:, :ROW_NEW].astype(jnp.bfloat16).reshape(8, ROW_NEW * LANES)

    def linear(i_y, i_x, i_z, i_c):
        return ((i_y * 4 + i_x) * 4 + i_z) * 2 + i_c

    def moves(by, first):
        pairs = []
        for i_y in range(4):
            for i_x in range(4):
                for i_z in range(4):
                    for i_c in range(2):
                        along_x = (i_c == 0) == first
                        to_y = i_y if along_x else (i_y + by) % 4
                        to_x = (i_x + by) % 4 if along_x else i_x
                        pairs.append((linear(i_y, i_x, i_z, i_c), linear(to_y, to_x, i_z, i_c)))
        return pairs

    def turn(value, first):
        return [value] + [
            lax.ppermute(value, ("y", "x", "z", "c"), moves(by, first)) for by in TURNS[1:]
        ]

    held = turn(jnp.stack(turn(mine, True)), False)
    params = pl.pallas_call(
        place_kernel,
        out_shape=jax.ShapeDtypeStruct((16, 8, ROW_NEW * LANES), jnp.bfloat16),
        in_specs=[vmem] * 4,
        out_specs=vmem,
        compiler_params=pltpu.CompilerParams(vmem_limit_bytes=16 * 1024 * 1024),
    )(*held).reshape(128, ROW_NEW * LANES)

    outs = pl.pallas_call(
        owner_kernel,
        out_shape=(jax.ShapeDtypeStruct((1, SLOT, LANES), jnp.float32),) * 3,
        in_specs=[smem, vmem, vmem],
        out_specs=(vmem, vmem, vmem),
        scratch_shapes=[pltpu.VMEM((3, 2 * SLOT, LANES), jnp.float32)],
        compiler_params=pltpu.CompilerParams(vmem_limit_bytes=24 * 1024 * 1024),
    )(new_table.T, block.astype(jnp.float32), grad)
    return (*outs, params)


def solution(mesh):
    fine = Mesh(mesh.devices.reshape(4, 4, 4, 2), ("y", "x", "z", "c"))
    parts = P(("y", "x", "z", "c"), None, None)
    return jax.shard_map(
        on_device,
        mesh=fine,
        in_specs=(parts, parts, parts, parts, P(), P(), P()),
        out_specs=(parts, parts, parts, P(None, ("z", "c"))),
        check_vma=False,
    )
```

```python
import functools
import jax
import jax.numpy as jnp
from jax import lax
from jax.experimental import pallas as pl
from jax.experimental.pallas import tpu as pltpu
from jax.sharding import Mesh, PartitionSpec as P

OLD_TP = 4
STEPS_DONE = 10
SLOT = 672
UNIT = 336
LANES = 128
ROW_OLD = 84
QUART = 21
QPAD = 24
ROW_NEW = 42
RPAD = 48
PAIR = 88
TURNS = (0, 2, 1, 3)

beta_first = 0.9
beta_second = 0.95
learn_rate = 0.1
decay_rate = 0.1
epsilon_add = 1e-08

SCALE_W = 2.0**13
SCALE_M = 2.0**15
SCALE_V = 2.0**15
SCALE_G = 2.0**13


def adam_update(master, moment, square, gradient):
    moment_new = beta_first * moment + (1.0 - beta_first) * gradient
    square_new = beta_second * square + (1.0 - beta_second) * gradient * gradient
    moment_hat = moment_new / (1.0 - beta_first**STEPS_DONE)
    square_hat = square_new / (1.0 - beta_second**STEPS_DONE)
    master_new = master - learn_rate * (
        moment_hat / (jnp.sqrt(square_hat) + epsilon_add) + decay_rate * master
    )
    return (master_new, moment_new, square_new)


def wrap(value):
    return jnp.where(value < 0, value + SLOT, value)


def pack_kernel(
    old_hbm, new_hbm, w_ref, m_ref, v_ref, g_ref, out_ref, gout_ref, info_ref,
    scratch, old_ref, new_ref, sems,
):
    tables = [
        pltpu.make_async_copy(old_hbm, old_ref, sems.at[4]),
        pltpu.make_async_copy(new_hbm, new_ref, sems.at[5]),
    ]
    for copy in tables:
        copy.start()
    copies = [
        pltpu.make_async_copy(ref.at[0], scratch.at[s, pl.ds(0, SLOT)], sems.at[s])
        for s, ref in enumerate((g_ref, w_ref, m_ref, v_ref))
    ]
    for copy in copies:
        copy.start()
    for copy in tables:
        copy.wait()
    dp = lax.axis_index("y") * 4 + lax.axis_index("x")
    tp = lax.axis_index("z") * 2 + lax.axis_index("c")
    old_start = lax.rem(old_ref[1, dp * 8 + tp], SLOT)
    new_start = new_ref[1, dp * 8 + tp]
    new_place = lax.rem(new_start - dp * UNIT, SLOT)
    above = lax.rem(dp + 1, 16)
    info_ref[0] = jnp.full((8, LANES), new_ref[1, above * 8 + tp] - above * UNIT, jnp.int32)
    info_ref[1] = jnp.full((8, LANES), new_start - above * UNIT, jnp.int32)
    for s, copy in enumerate(copies):
        copy.wait()
        scratch[s, pl.ds(SLOT, RPAD), :] = scratch[s, pl.ds(0, RPAD), :]
        if s == 0:
            for half in range(2):
                for t in range(8):
                    offset = wrap(half * UNIT + t * ROW_NEW - new_place)
                    gout_ref[half, t] = scratch[0, pl.ds(offset, RPAD), :] * SCALE_G
            continue
        scale = (SCALE_W, SCALE_M, SCALE_V)[s - 1]
        for hq in range(4):
            for t in range(8):
                offset = wrap(t * ROW_OLD + hq * QUART - old_start)
                piece = scratch[s, pl.ds(offset, QPAD), :]
                out_ref[hq * 8 + t, :, pl.ds((s - 1) * LANES, LANES)] = piece * scale


def owner_kernel(new_ref, rows_ref, g_ref, w_out, m_out, v_out, scratch):
    dp = lax.axis_index("y") * 4 + lax.axis_index("x")
    tp = lax.axis_index("z") * 2 + lax.axis_index("c")
    new_place = lax.rem(new_ref[1, dp * 8 + tp] - dp * UNIT, SLOT)
    length = new_ref[2, dp * 8 + tp]
    for half in range(2):
        for t in range(8):
            for s in range(3):
                piece = rows_ref[t, pl.ds((1 - half) * ROW_NEW, ROW_NEW), pl.ds(s * LANES, LANES)]
                at = half * UNIT + t * ROW_NEW
                scratch[s, pl.ds(at, ROW_NEW), :] = piece
                scratch[s, pl.ds(at + SLOT, ROW_NEW), :] = piece
    step = 96
    for c in range(SLOT // step):
        at = new_place + c * step
        w = scratch[0, pl.ds(at, step), :] * (1.0 / SCALE_W)
        m = scratch[1, pl.ds(at, step), :] * (1.0 / SCALE_M)
        v = scratch[2, pl.ds(at, step), :] * (1.0 / SCALE_V)
        rows = pl.ds(c * step, step)
        slot = lax.broadcasted_iota(jnp.int32, (step, LANES), 0) + c * step
        inside = slot < length
        new = adam_update(w, m, v, g_ref[0, rows, :])
        for ref, value in zip((w_out, m_out, v_out), new):
            ref[0, rows, :] = jnp.where(inside, value, 0.0)


def place_kernel(*refs):
    held, out_ref = refs[:4], refs[4]
    y, x = lax.axis_index("y"), lax.axis_index("x")
    x_first = lax.axis_index("c") == 0
    for k in range(4):
        for l in range(4):
            dy = jnp.where(x_first, TURNS[k], TURNS[l])
            dx = jnp.where(x_first, TURNS[l], TURNS[k])
            block = lax.rem(lax.rem(y + 4 - dy, 4) * 4 + lax.rem(x + 4 - dx, 4) + 1, 16)
            out_ref[block] = held[k][l]


def one_hot_dot(chosen, source):
    picked = jnp.dot(
        chosen.astype(jnp.float32),
        source.astype(jnp.float32),
        precision=lax.Precision.HIGH,
        preferred_element_type=jnp.float32,
    )
    return picked.astype(jnp.float16)


def on_device(old_master, old_avg, old_sq, grad, old_table, new_table, head_order):
    y = lax.axis_index("y")
    x = lax.axis_index("x")
    core = lax.axis_index("c")
    t = lax.axis_index("z") * 2 + core
    dp = y * 4 + x
    f16 = jnp.float16

    vmem = pl.BlockSpec(memory_space=pltpu.VMEM)
    smem = pl.BlockSpec(memory_space=pltpu.SMEM)
    hbm = pl.BlockSpec(memory_space=pltpu.HBM)
    packed, grad_rows, info = pl.pallas_call(
        pack_kernel,
        out_shape=(
            pltpu.VMEM((32, QPAD, 3 * LANES), jnp.float32),
            pltpu.VMEM((2, 8, RPAD, LANES), jnp.float32),
            pltpu.VMEM((2, 8, LANES), jnp.int32),
        ),
        in_specs=[hbm] * 6,
        out_specs=(vmem, vmem, vmem),
        scratch_shapes=[
            pltpu.VMEM((4, SLOT + RPAD, LANES), jnp.float32),
            pltpu.SMEM((3, 128), jnp.int32),
            pltpu.SMEM((3, 128), jnp.int32),
            pltpu.SemaphoreType.DMA((6,)),
        ],
    )(old_table.T, new_table.T, old_master, old_avg, old_sq, grad)

    up = [(i, (i + 1) % 16) for i in range(16)]
    down = [(i, (i - 1) % 16) for i in range(16)]

    first = lax.all_to_all(packed.astype(f16), ("x", "z", "c"), 0, 0, tiled=True)

    grad_rows, first = lax.optimization_barrier((grad_rows, first))
    grad_send = grad_rows.astype(f16)
    grad_first = lax.ppermute(grad_send[0], ("y", "x"), down)
    grad_last = lax.ppermute(grad_send[0], ("y", "x"), up)

    ranks = lax.dynamic_slice_in_dim(old_table, y * 32, 32, 0)
    begin = jnp.broadcast_to(ranks[:, 1:2], (32, QPAD)).reshape(1, 32 * QPAD)
    end = begin + jnp.broadcast_to(ranks[:, 2:3], (32, QPAD)).reshape(1, 32 * QPAD)
    heads_here = y * 28 + x * 7 + jnp.arange(7, dtype=jnp.int32)
    at_head = head_order[None, :] == heads_here[:, None]
    position = jnp.sum(jnp.where(at_head, jnp.arange(112, dtype=jnp.int32)[None, :], 0), axis=1)
    rank_new, j_new = position // 14, position % 14
    starts = new_table[:, 1].reshape(16, 1, 8)
    at_rank = rank_new[None, :, None] == jnp.arange(8, dtype=jnp.int32)[None, None, :]
    edge = jnp.sum(jnp.where(at_rank, starts, 0), axis=2)
    e = jnp.arange(16, dtype=jnp.int32)
    edge = edge - e[:, None] * UNIT - t * ROW_NEW - j_new[None, :]
    near = 14 * jnp.arange(3, dtype=jnp.int32)[None, None, :] >= edge[:, :, None]
    near = jnp.pad(near.reshape(16, QUART), ((0, 0), (0, QPAD - QUART)))
    block_end = jnp.where(near, e[:, None], (e[:, None] + 2) % 16)
    block_own = jnp.broadcast_to((e[:, None] + 1) % 16, (16, QPAD))
    source = jnp.stack([block_own, block_end], axis=1)
    j = jnp.arange(QPAD, dtype=jnp.int32)[None, None, :]
    flat = (source * 8 + t) * ROW_OLD + x * QUART + j
    flat = jnp.where(j < QUART, flat, -1).reshape(32 * QPAD, 1)
    row_id = lax.broadcasted_iota(jnp.int32, (32 * QPAD, 32 * QPAD), 0)
    col_id = lax.broadcasted_iota(jnp.int32, (32 * QPAD, 32 * QPAD), 1)
    chosen = (row_id % QPAD == col_id % QPAD) & (flat >= begin) & (flat < end)
    chosen = lax.optimization_barrier(chosen.astype(jnp.bfloat16))
    rows = one_hot_dot(chosen, first.reshape(32 * QPAD, 3 * LANES))

    second = lax.all_to_all(
        rows.reshape(16, 2 * QPAD, 3 * LANES), ("y", "x"), 0, 0, tiled=True
    )
    second, grad_first = lax.optimization_barrier((second, grad_first))
    order = head_order.reshape(8, 1, 1, 14)
    kind = jnp.arange(2, dtype=jnp.int32).reshape(1, 2, 1, 1)
    comp = jnp.arange(3, dtype=jnp.int32).reshape(1, 1, 3, 1)
    origin = ((order // 7) * 2 + kind) * QPAD + (order % 7) * 3 + comp
    origin = jnp.pad(origin.reshape(8, 2 * ROW_NEW), ((0, 0), (0, PAIR - 2 * ROW_NEW)))
    origin = origin.reshape(8 * PAIR, 1)
    col_id = lax.broadcasted_iota(jnp.int32, (8 * PAIR, 32 * QPAD), 1)
    moved = lax.optimization_barrier((origin == col_id).astype(jnp.bfloat16))
    heads = one_hot_dot(moved, second.reshape(32 * QPAD, 3 * LANES))

    block = lax.all_to_all(heads.reshape(8, PAIR, 3 * LANES), ("z", "c"), 0, 0, tiled=True)

    own = lax.broadcasted_iota(jnp.int32, (8, RPAD, LANES), 0) * ROW_NEW
    own = own + lax.broadcasted_iota(jnp.int32, (8, RPAD, LANES), 1)
    gradient = jnp.where(
        own >= info[0, 0],
        grad_first.astype(jnp.float32),
        jnp.where(
            own >= info[1, 0],
            grad_send[1].astype(jnp.float32),
            grad_last.astype(jnp.float32),
        ),
    ) * (1.0 / SCALE_G)
    wide = block[:, :RPAD].astype(jnp.float32)
    master, _, _ = adam_update(
        wide[:, :, :LANES] * (1.0 / SCALE_W),
        wide[:, :, LANES : 2 * LANES] * (1.0 / SCALE_M),
        wide[:, :, 2 * LANES :] * (1.0 / SCALE_V),
        gradient,
    )
    mine = master[:, :ROW_NEW].astype(jnp.bfloat16).reshape(8, ROW_NEW * LANES)

    def linear(i_y, i_x, i_z, i_c):
        return ((i_y * 4 + i_x) * 4 + i_z) * 2 + i_c

    def moves(by, first):
        pairs = []
        for i_y in range(4):
            for i_x in range(4):
                for i_z in range(4):
                    for i_c in range(2):
                        along_x = (i_c == 0) == first
                        to_y = i_y if along_x else (i_y + by) % 4
                        to_x = (i_x + by) % 4 if along_x else i_x
                        pairs.append((linear(i_y, i_x, i_z, i_c), linear(to_y, to_x, i_z, i_c)))
        return pairs

    def turn(value, first):
        return [value] + [
            lax.ppermute(value, ("y", "x", "z", "c"), moves(by, first)) for by in TURNS[1:]
        ]

    held = turn(jnp.stack(turn(mine, True)), False)
    params = pl.pallas_call(
        place_kernel,
        out_shape=jax.ShapeDtypeStruct((16, 8, ROW_NEW * LANES), jnp.bfloat16),
        in_specs=[vmem] * 4,
        out_specs=vmem,
        compiler_params=pltpu.CompilerParams(vmem_limit_bytes=16 * 1024 * 1024),
    )(*held).reshape(128, ROW_NEW * LANES)

    outs = pl.pallas_call(
        owner_kernel,
        out_shape=(jax.ShapeDtypeStruct((1, SLOT, LANES), jnp.float32),) * 3,
        in_specs=[smem, vmem, vmem],
        out_specs=(vmem, vmem, vmem),
        scratch_shapes=[pltpu.VMEM((3, 2 * SLOT, LANES), jnp.float32)],
        compiler_params=pltpu.CompilerParams(vmem_limit_bytes=24 * 1024 * 1024),
    )(new_table.T, block.astype(jnp.float32), grad)
    return (*outs, params)


def solution(mesh):
    fine = Mesh(mesh.devices.reshape(4, 4, 4, 2), ("y", "x", "z", "c"))
    parts = P(("y", "x", "z", "c"), None, None)
    return jax.shard_map(
        on_device,
        mesh=fine,
        in_specs=(parts, parts, parts, parts, P(), P(), P()),
        out_specs=(parts, parts, parts, P(None, ("z", "c"))),
        check_vma=False,
    )
```

```python
import functools
import jax
import jax.numpy as jnp
from jax import lax
from jax.experimental import pallas as pl
from jax.experimental.pallas import tpu as pltpu
from jax.sharding import Mesh, PartitionSpec as P

OLD_TP = 4
STEPS_DONE = 10
SLOT = 672
UNIT = 336
LANES = 128
ROW_OLD = 84
QUART = 21
QPAD = 24
ROW_NEW = 42
RPAD = 48
PAIR = 88
TURNS = (0, 2, 1, 3)

beta_first = 0.9
beta_second = 0.95
learn_rate = 0.1
decay_rate = 0.1
epsilon_add = 1e-08

SCALE_W = 2.0**13
SCALE_M = 2.0**15
SCALE_V = 2.0**15
SCALE_G = 2.0**13


def adam_update(master, moment, square, gradient):
    moment_new = beta_first * moment + (1.0 - beta_first) * gradient
    square_new = beta_second * square + (1.0 - beta_second) * gradient * gradient
    moment_hat = moment_new / (1.0 - beta_first**STEPS_DONE)
    square_hat = square_new / (1.0 - beta_second**STEPS_DONE)
    master_new = master - learn_rate * (
        moment_hat / (jnp.sqrt(square_hat) + epsilon_add) + decay_rate * master
    )
    return (master_new, moment_new, square_new)


def wrap(value):
    return jnp.where(value < 0, value + SLOT, value)


def pack_kernel(
    old_hbm, w_ref, m_ref, v_ref, out_ref, scratch, old_ref, sems
):
    table = pltpu.make_async_copy(old_hbm, old_ref, sems.at[3])
    table.start()
    copies = [
        pltpu.make_async_copy(ref.at[0], scratch.at[s, pl.ds(0, SLOT)], sems.at[s])
        for s, ref in enumerate((w_ref, m_ref, v_ref))
    ]
    for copy in copies:
        copy.start()
    table.wait()
    dp = lax.axis_index("y") * 4 + lax.axis_index("x")
    tp = lax.axis_index("z") * 2 + lax.axis_index("c")
    old_start = lax.rem(old_ref[1, dp * 8 + tp], SLOT)
    for s, copy in enumerate(copies):
        copy.wait()
        scratch[s, pl.ds(SLOT, QPAD), :] = scratch[s, pl.ds(0, QPAD), :]
        scale = (SCALE_W, SCALE_M, SCALE_V)[s]
        for hq in range(4):
            for t in range(8):
                offset = wrap(t * ROW_OLD + hq * QUART - old_start)
                piece = scratch[s, pl.ds(offset, QPAD), :]
                out_ref[hq * 8 + t, :, pl.ds(s * LANES, LANES)] = piece * scale


def grad_kernel(new_ref, g_ref, gout_ref, info_ref, scratch):
    dp = lax.axis_index("y") * 4 + lax.axis_index("x")
    tp = lax.axis_index("z") * 2 + lax.axis_index("c")
    new_start = new_ref[1, dp * 8 + tp]
    new_place = lax.rem(new_start - dp * UNIT, SLOT)
    above = lax.rem(dp + 1, 16)
    info_ref[0] = jnp.full((8, LANES), new_ref[1, above * 8 + tp] - above * UNIT, jnp.int32)
    info_ref[1] = jnp.full((8, LANES), new_start - above * UNIT, jnp.int32)
    scratch[pl.ds(0, SLOT), :] = g_ref[0]
    scratch[pl.ds(SLOT, RPAD), :] = g_ref[0, pl.ds(0, RPAD), :]
    for half in range(2):
        for t in range(8):
            offset = wrap(half * UNIT + t * ROW_NEW - new_place)
            gout_ref[half, t] = scratch[pl.ds(offset, RPAD), :] * SCALE_G


def owner_kernel(new_ref, rows_ref, g_ref, w_out, m_out, v_out, scratch):
    dp = lax.axis_index("y") * 4 + lax.axis_index("x")
    tp = lax.axis_index("z") * 2 + lax.axis_index("c")
    new_place = lax.rem(new_ref[1, dp * 8 + tp] - dp * UNIT, SLOT)
    length = new_ref[2, dp * 8 + tp]
    for half in range(2):
        for t in range(8):
            for s in range(3):
                piece = rows_ref[t, pl.ds((1 - half) * ROW_NEW, ROW_NEW), pl.ds(s * LANES, LANES)]
                at = half * UNIT + t * ROW_NEW
                scratch[s, pl.ds(at, ROW_NEW), :] = piece
                scratch[s, pl.ds(at + SLOT, ROW_NEW), :] = piece
    step = 96
    for c in range(SLOT // step):
        at = new_place + c * step
        w = scratch[0, pl.ds(at, step), :] * (1.0 / SCALE_W)
        m = scratch[1, pl.ds(at, step), :] * (1.0 / SCALE_M)
        v = scratch[2, pl.ds(at, step), :] * (1.0 / SCALE_V)
        rows = pl.ds(c * step, step)
        slot = lax.broadcasted_iota(jnp.int32, (step, LANES), 0) + c * step
        inside = slot < length
        new = adam_update(w, m, v, g_ref[0, rows, :])
        for ref, value in zip((w_out, m_out, v_out), new):
            ref[0, rows, :] = jnp.where(inside, value, 0.0)


def place_kernel(*refs):
    held, out_ref = refs[:4], refs[4]
    y, x = lax.axis_index("y"), lax.axis_index("x")
    x_first = lax.axis_index("c") == 0
    for k in range(4):
        for l in range(4):
            dy = jnp.where(x_first, TURNS[k], TURNS[l])
            dx = jnp.where(x_first, TURNS[l], TURNS[k])
            block = lax.rem(lax.rem(y + 4 - dy, 4) * 4 + lax.rem(x + 4 - dx, 4) + 1, 16)
            out_ref[block] = held[k][l]


def one_hot_dot(chosen, source):
    picked = jnp.dot(
        chosen.astype(jnp.float32),
        source.astype(jnp.float32),
        precision=lax.Precision.HIGH,
        preferred_element_type=jnp.float32,
    )
    return picked.astype(jnp.float16)


def on_device(old_master, old_avg, old_sq, grad, old_table, new_table, head_order):
    y = lax.axis_index("y")
    x = lax.axis_index("x")
    core = lax.axis_index("c")
    t = lax.axis_index("z") * 2 + core
    dp = y * 4 + x
    f16 = jnp.float16

    vmem = pl.BlockSpec(memory_space=pltpu.VMEM)
    smem = pl.BlockSpec(memory_space=pltpu.SMEM)
    hbm = pl.BlockSpec(memory_space=pltpu.HBM)
    packed = pl.pallas_call(
        pack_kernel,
        out_shape=pltpu.VMEM((32, QPAD, 3 * LANES), jnp.float32),
        in_specs=[hbm] * 4,
        out_specs=vmem,
        scratch_shapes=[
            pltpu.VMEM((3, SLOT + RPAD, LANES), jnp.float32),
            pltpu.SMEM((3, 128), jnp.int32),
            pltpu.SemaphoreType.DMA((4,)),
        ],
    )(old_table.T, old_master, old_avg, old_sq)
    grad_rows, info = pl.pallas_call(
        grad_kernel,
        out_shape=(
            jax.ShapeDtypeStruct((2, 8, RPAD, LANES), jnp.float32),
            jax.ShapeDtypeStruct((2, 8, LANES), jnp.int32),
        ),
        in_specs=[smem, vmem],
        out_specs=(vmem, vmem),
        scratch_shapes=[pltpu.VMEM((SLOT + RPAD, LANES), jnp.float32)],
        compiler_params=pltpu.CompilerParams(vmem_limit_bytes=16 * 1024 * 1024),
    )(new_table.T, grad)

    up = [(i, (i + 1) % 16) for i in range(16)]
    down = [(i, (i - 1) % 16) for i in range(16)]

    first = lax.all_to_all(packed.astype(f16), ("x", "z", "c"), 0, 0, tiled=True)

    grad_rows, first = lax.optimization_barrier((grad_rows, first))
    grad_send = grad_rows.astype(f16)
    grad_first = lax.ppermute(grad_send[0], ("y", "x"), down)
    grad_last = lax.ppermute(grad_send[0], ("y", "x"), up)

    ranks = lax.dynamic_slice_in_dim(old_table, y * 32, 32, 0)
    begin = jnp.broadcast_to(ranks[:, 1:2], (32, QPAD)).reshape(1, 32 * QPAD)
    end = begin + jnp.broadcast_to(ranks[:, 2:3], (32, QPAD)).reshape(1, 32 * QPAD)
    heads_here = y * 28 + x * 7 + jnp.arange(7, dtype=jnp.int32)
    at_head = head_order[None, :] == heads_here[:, None]
    position = jnp.sum(jnp.where(at_head, jnp.arange(112, dtype=jnp.int32)[None, :], 0), axis=1)
    rank_new, j_new = position // 14, position % 14
    starts = new_table[:, 1].reshape(16, 1, 8)
    at_rank = rank_new[None, :, None] == jnp.arange(8, dtype=jnp.int32)[None, None, :]
    edge = jnp.sum(jnp.where(at_rank, starts, 0), axis=2)
    e = jnp.arange(16, dtype=jnp.int32)
    edge = edge - e[:, None] * UNIT - t * ROW_NEW - j_new[None, :]
    near = 14 * jnp.arange(3, dtype=jnp.int32)[None, None, :] >= edge[:, :, None]
    near = jnp.pad(near.reshape(16, QUART), ((0, 0), (0, QPAD - QUART)))
    block_end = jnp.where(near, e[:, None], (e[:, None] + 2) % 16)
    block_own = jnp.broadcast_to((e[:, None] + 1) % 16, (16, QPAD))
    source = jnp.stack([block_own, block_end], axis=1)
    j = jnp.arange(QPAD, dtype=jnp.int32)[None, None, :]
    flat = (source * 8 + t) * ROW_OLD + x * QUART + j
    flat = jnp.where(j < QUART, flat, -1).reshape(32 * QPAD, 1)
    row_id = lax.broadcasted_iota(jnp.int32, (32 * QPAD, 32 * QPAD), 0)
    col_id = lax.broadcasted_iota(jnp.int32, (32 * QPAD, 32 * QPAD), 1)
    chosen = (row_id % QPAD == col_id % QPAD) & (flat >= begin) & (flat < end)
    chosen = lax.optimization_barrier(chosen.astype(jnp.bfloat16))
    rows = one_hot_dot(chosen, first.reshape(32 * QPAD, 3 * LANES))

    second = lax.all_to_all(
        rows.reshape(16, 2 * QPAD, 3 * LANES), ("y", "x"), 0, 0, tiled=True
    )
    second, grad_first = lax.optimization_barrier((second, grad_first))
    order = head_order.reshape(8, 1, 1, 14)
    kind = jnp.arange(2, dtype=jnp.int32).reshape(1, 2, 1, 1)
    comp = jnp.arange(3, dtype=jnp.int32).reshape(1, 1, 3, 1)
    origin = ((order // 7) * 2 + kind) * QPAD + (order % 7) * 3 + comp
    origin = jnp.pad(origin.reshape(8, 2 * ROW_NEW), ((0, 0), (0, PAIR - 2 * ROW_NEW)))
    origin = origin.reshape(8 * PAIR, 1)
    col_id = lax.broadcasted_iota(jnp.int32, (8 * PAIR, 32 * QPAD), 1)
    moved = lax.optimization_barrier((origin == col_id).astype(jnp.bfloat16))
    heads = one_hot_dot(moved, second.reshape(32 * QPAD, 3 * LANES))

    block = lax.all_to_all(heads.reshape(8, PAIR, 3 * LANES), ("z", "c"), 0, 0, tiled=True)

    own = lax.broadcasted_iota(jnp.int32, (8, RPAD, LANES), 0) * ROW_NEW
    own = own + lax.broadcasted_iota(jnp.int32, (8, RPAD, LANES), 1)
    gradient = jnp.where(
        own >= info[0, 0],
        grad_first.astype(jnp.float32),
        jnp.where(
            own >= info[1, 0],
            grad_send[1].astype(jnp.float32),
            grad_last.astype(jnp.float32),
        ),
    ) * (1.0 / SCALE_G)
    wide = block[:, :RPAD].astype(jnp.float32)
    master, _, _ = adam_update(
        wide[:, :, :LANES] * (1.0 / SCALE_W),
        wide[:, :, LANES : 2 * LANES] * (1.0 / SCALE_M),
        wide[:, :, 2 * LANES :] * (1.0 / SCALE_V),
        gradient,
    )
    mine = master[:, :ROW_NEW].astype(jnp.bfloat16).reshape(8, ROW_NEW * LANES)

    def linear(i_y, i_x, i_z, i_c):
        return ((i_y * 4 + i_x) * 4 + i_z) * 2 + i_c

    def moves(by, first):
        pairs = []
        for i_y in range(4):
            for i_x in range(4):
                for i_z in range(4):
                    for i_c in range(2):
                        along_x = (i_c == 0) == first
                        to_y = i_y if along_x else (i_y + by) % 4
                        to_x = (i_x + by) % 4 if along_x else i_x
                        pairs.append((linear(i_y, i_x, i_z, i_c), linear(to_y, to_x, i_z, i_c)))
        return pairs

    def turn(value, first):
        return [value] + [
            lax.ppermute(value, ("y", "x", "z", "c"), moves(by, first)) for by in TURNS[1:]
        ]

    held = turn(jnp.stack(turn(mine, True)), False)
    params = pl.pallas_call(
        place_kernel,
        out_shape=jax.ShapeDtypeStruct((16, 8, ROW_NEW * LANES), jnp.bfloat16),
        in_specs=[vmem] * 4,
        out_specs=vmem,
        compiler_params=pltpu.CompilerParams(vmem_limit_bytes=16 * 1024 * 1024),
    )(*held).reshape(128, ROW_NEW * LANES)

    outs = pl.pallas_call(
        owner_kernel,
        out_shape=(jax.ShapeDtypeStruct((1, SLOT, LANES), jnp.float32),) * 3,
        in_specs=[smem, vmem, vmem],
        out_specs=(vmem, vmem, vmem),
        scratch_shapes=[pltpu.VMEM((3, 2 * SLOT, LANES), jnp.float32)],
        compiler_params=pltpu.CompilerParams(vmem_limit_bytes=24 * 1024 * 1024),
    )(new_table.T, block.astype(jnp.float32), grad)
    return (*outs, params)


def solution(mesh):
    fine = Mesh(mesh.devices.reshape(4, 4, 4, 2), ("y", "x", "z", "c"))
    parts = P(("y", "x", "z", "c"), None, None)
    return jax.shard_map(
        on_device,
        mesh=fine,
        in_specs=(parts, parts, parts, parts, P(), P(), P()),
        out_specs=(parts, parts, parts, P(None, ("z", "c"))),
        check_vma=False,
    )
```

```python
import functools
import jax
import jax.numpy as jnp
from jax import lax
from jax.experimental import pallas as pl
from jax.experimental.pallas import tpu as pltpu
from jax.sharding import Mesh, PartitionSpec as P

OLD_TP = 4
STEPS_DONE = 10
SLOT = 672
UNIT = 336
LANES = 128
ROW_OLD = 84
QUART = 21
QPAD = 24
ROW_NEW = 42
RPAD = 48
TURNS = (0, 2, 1, 3)

beta_first = 0.9
beta_second = 0.95
learn_rate = 0.1
decay_rate = 0.1
epsilon_add = 1e-08

SCALE_W = 2.0**13
SCALE_M = 2.0**15
SCALE_V = 2.0**15
SCALE_G = 2.0**13


def adam_update(master, moment, square, gradient):
    moment_new = beta_first * moment + (1.0 - beta_first) * gradient
    square_new = beta_second * square + (1.0 - beta_second) * gradient * gradient
    moment_hat = moment_new / (1.0 - beta_first**STEPS_DONE)
    square_hat = square_new / (1.0 - beta_second**STEPS_DONE)
    master_new = master - learn_rate * (
        moment_hat / (jnp.sqrt(square_hat) + epsilon_add) + decay_rate * master
    )
    return (master_new, moment_new, square_new)


def wrap(value):
    return jnp.where(value < 0, value + SLOT, value)


def pack_kernel(
    old_hbm, w_ref, m_ref, v_ref, out_ref, scratch, old_ref, sems
):
    table = pltpu.make_async_copy(old_hbm, old_ref, sems.at[3])
    table.start()
    copies = [
        pltpu.make_async_copy(ref.at[0], scratch.at[s, pl.ds(0, SLOT)], sems.at[s])
        for s, ref in enumerate((w_ref, m_ref, v_ref))
    ]
    for copy in copies:
        copy.start()
    table.wait()
    dp = lax.axis_index("y") * 4 + lax.axis_index("x")
    tp = lax.axis_index("z") * 2 + lax.axis_index("c")
    old_start = lax.rem(old_ref[1, dp * 8 + tp], SLOT)
    for s, copy in enumerate(copies):
        copy.wait()
        scratch[s, pl.ds(SLOT, QPAD), :] = scratch[s, pl.ds(0, QPAD), :]
        scale = (SCALE_W, SCALE_M, SCALE_V)[s]
        for hq in range(4):
            for t in range(8):
                offset = wrap(t * ROW_OLD + hq * QUART - old_start)
                piece = scratch[s, pl.ds(offset, QPAD), :]
                out_ref[hq * 8 + t, :, pl.ds(s * LANES, LANES)] = piece * scale


def grad_kernel(new_ref, g_ref, gout_ref, info_ref, scratch):
    dp = lax.axis_index("y") * 4 + lax.axis_index("x")
    tp = lax.axis_index("z") * 2 + lax.axis_index("c")
    new_start = new_ref[1, dp * 8 + tp]
    new_place = lax.rem(new_start - dp * UNIT, SLOT)
    above = lax.rem(dp + 1, 16)
    info_ref[0] = jnp.full((8, LANES), new_ref[1, above * 8 + tp] - above * UNIT, jnp.int32)
    info_ref[1] = jnp.full((8, LANES), new_start - above * UNIT, jnp.int32)
    scratch[pl.ds(0, SLOT), :] = g_ref[0]
    scratch[pl.ds(SLOT, RPAD), :] = g_ref[0, pl.ds(0, RPAD), :]
    for half in range(2):
        for t in range(8):
            offset = wrap(half * UNIT + t * ROW_NEW - new_place)
            gout_ref[half, t] = scratch[pl.ds(offset, RPAD), :] * SCALE_G


def owner_kernel(new_ref, ends_ref, mid_ref, g_ref, w_out, m_out, v_out, scratch):
    dp = lax.axis_index("y") * 4 + lax.axis_index("x")
    tp = lax.axis_index("z") * 2 + lax.axis_index("c")
    new_place = lax.rem(new_ref[1, dp * 8 + tp] - dp * UNIT, SLOT)
    length = new_ref[2, dp * 8 + tp]
    for half, ref in enumerate((ends_ref, mid_ref)):
        for t in range(8):
            for s in range(3):
                piece = ref[t, pl.ds(0, ROW_NEW), pl.ds(s * LANES, LANES)]
                at = half * UNIT + t * ROW_NEW
                scratch[s, pl.ds(at, ROW_NEW), :] = piece
                scratch[s, pl.ds(at + SLOT, ROW_NEW), :] = piece
    step = 96
    for c in range(SLOT // step):
        at = new_place + c * step
        w = scratch[0, pl.ds(at, step), :] * (1.0 / SCALE_W)
        m = scratch[1, pl.ds(at, step), :] * (1.0 / SCALE_M)
        v = scratch[2, pl.ds(at, step), :] * (1.0 / SCALE_V)
        rows = pl.ds(c * step, step)
        slot = lax.broadcasted_iota(jnp.int32, (step, LANES), 0) + c * step
        inside = slot < length
        new = adam_update(w, m, v, g_ref[0, rows, :])
        for ref, value in zip((w_out, m_out, v_out), new):
            ref[0, rows, :] = jnp.where(inside, value, 0.0)


def place_kernel(*refs):
    held, out_ref = refs[:4], refs[4]
    y, x = lax.axis_index("y"), lax.axis_index("x")
    x_first = lax.axis_index("c") == 0
    for k in range(4):
        for l in range(4):
            dy = jnp.where(x_first, TURNS[k], TURNS[l])
            dx = jnp.where(x_first, TURNS[l], TURNS[k])
            block = lax.rem(lax.rem(y + 4 - dy, 4) * 4 + lax.rem(x + 4 - dx, 4) + 1, 16)
            out_ref[block] = held[k][l]


def one_hot_dot(chosen, source):
    picked = jnp.dot(
        chosen.astype(jnp.float32),
        source.astype(jnp.float32),
        precision=lax.Precision.HIGH,
        preferred_element_type=jnp.float32,
    )
    return picked.astype(jnp.float16)


def on_device(old_master, old_avg, old_sq, grad, old_table, new_table, head_order):
    y = lax.axis_index("y")
    x = lax.axis_index("x")
    core = lax.axis_index("c")
    z = lax.axis_index("z")
    t = z * 2 + core
    dp = y * 4 + x
    f16 = jnp.float16

    vmem = pl.BlockSpec(memory_space=pltpu.VMEM)
    smem = pl.BlockSpec(memory_space=pltpu.SMEM)
    hbm = pl.BlockSpec(memory_space=pltpu.HBM)
    packed = pl.pallas_call(
        pack_kernel,
        out_shape=pltpu.VMEM((32, QPAD, 3 * LANES), jnp.float32),
        in_specs=[hbm] * 4,
        out_specs=vmem,
        scratch_shapes=[
            pltpu.VMEM((3, SLOT + RPAD, LANES), jnp.float32),
            pltpu.SMEM((3, 128), jnp.int32),
            pltpu.SemaphoreType.DMA((4,)),
        ],
    )(old_table.T, old_master, old_avg, old_sq)
    grad_rows, info = pl.pallas_call(
        grad_kernel,
        out_shape=(
            jax.ShapeDtypeStruct((2, 8, RPAD, LANES), jnp.float32),
            jax.ShapeDtypeStruct((2, 8, LANES), jnp.int32),
        ),
        in_specs=[smem, vmem],
        out_specs=(vmem, vmem),
        scratch_shapes=[pltpu.VMEM((SLOT + RPAD, LANES), jnp.float32)],
        compiler_params=pltpu.CompilerParams(vmem_limit_bytes=16 * 1024 * 1024),
    )(new_table.T, grad)

    up = [(i, (i + 1) % 16) for i in range(16)]
    down = [(i, (i - 1) % 16) for i in range(16)]

    first = lax.all_to_all(packed.astype(f16), ("x", "z", "c"), 0, 0, tiled=True)

    grad_rows, first = lax.optimization_barrier((grad_rows, first))
    grad_send = grad_rows.astype(f16)
    grad_first = lax.ppermute(grad_send[0], ("y", "x"), down)
    grad_last = lax.ppermute(grad_send[0], ("y", "x"), up)

    ranks = lax.dynamic_slice_in_dim(old_table, y * 32, 32, 0)
    begin = jnp.broadcast_to(ranks[:, 1:2], (32, QPAD)).reshape(1, 32 * QPAD)
    end = begin + jnp.broadcast_to(ranks[:, 2:3], (32, QPAD)).reshape(1, 32 * QPAD)
    heads_here = y * 28 + x * 7 + jnp.arange(7, dtype=jnp.int32)
    at_head = head_order[None, :] == heads_here[:, None]
    position = jnp.sum(jnp.where(at_head, jnp.arange(112, dtype=jnp.int32)[None, :], 0), axis=1)
    rank_new, j_new = position // 14, position % 14
    starts = new_table[:, 1].reshape(16, 1, 8)
    at_rank = rank_new[None, :, None] == jnp.arange(8, dtype=jnp.int32)[None, None, :]
    edge = jnp.sum(jnp.where(at_rank, starts, 0), axis=2)
    e = jnp.arange(16, dtype=jnp.int32)
    edge = edge - e[:, None] * UNIT - t * ROW_NEW - j_new[None, :]
    near = 14 * jnp.arange(3, dtype=jnp.int32)[None, None, :] >= edge[:, :, None]
    near = jnp.pad(near.reshape(16, QUART), ((0, 0), (0, QPAD - QUART)))
    block_end = jnp.where(near, e[:, None], (e[:, None] + 2) % 16)
    block_own = jnp.broadcast_to((e[:, None] + 1) % 16, (16, QPAD))
    source = jnp.stack([block_own, block_end], axis=1)
    j = jnp.arange(QPAD, dtype=jnp.int32)[None, None, :]
    flat = (source * 8 + t) * ROW_OLD + x * QUART + j
    flat = jnp.where(j < QUART, flat, -1).reshape(32 * QPAD, 1)
    row_id = lax.broadcasted_iota(jnp.int32, (32 * QPAD, 32 * QPAD), 0)
    col_id = lax.broadcasted_iota(jnp.int32, (32 * QPAD, 32 * QPAD), 1)
    chosen = (row_id % QPAD == col_id % QPAD) & (flat >= begin) & (flat < end)
    chosen = lax.optimization_barrier(chosen.astype(jnp.bfloat16))
    rows = one_hot_dot(chosen, first.reshape(32 * QPAD, 3 * LANES))

    second = lax.all_to_all(
        rows.reshape(16, 2 * QPAD, 3 * LANES), ("y", "x"), 0, 0, tiled=True
    )
    second, grad_first, grad_last = lax.optimization_barrier((second, grad_first, grad_last))
    second = second.reshape(32 * QPAD, 3 * LANES)
    order = head_order.reshape(8, 1, 14)
    comp = jnp.arange(3, dtype=jnp.int32).reshape(1, 3, 1)
    origin = (order // 7) * (2 * QPAD) + (order % 7) * 3 + comp
    origin = jnp.pad(origin.reshape(8, ROW_NEW), ((0, 0), (0, RPAD - ROW_NEW)))
    origin = origin.reshape(8 * RPAD, 1)
    col_id = lax.broadcasted_iota(jnp.int32, (8 * RPAD, 32 * QPAD), 1)
    moved = lax.optimization_barrier((origin == col_id).astype(jnp.bfloat16))
    moved_ends = lax.optimization_barrier((origin + QPAD == col_id).astype(jnp.bfloat16))
    heads = one_hot_dot(moved, second).reshape(8, RPAD, 3 * LANES)

    block = lax.all_to_all(heads, ("z", "c"), 0, 0, tiled=True)

    own = lax.broadcasted_iota(jnp.int32, (8, RPAD, LANES), 0) * ROW_NEW
    own = own + lax.broadcasted_iota(jnp.int32, (8, RPAD, LANES), 1)
    gradient = jnp.where(
        own >= info[0, 0],
        grad_first.astype(jnp.float32),
        jnp.where(
            own >= info[1, 0],
            grad_send[1].astype(jnp.float32),
            grad_last.astype(jnp.float32),
        ),
    ) * (1.0 / SCALE_G)
    wide = block.astype(jnp.float32)
    master, _, _ = adam_update(
        wide[:, :, :LANES] * (1.0 / SCALE_W),
        wide[:, :, LANES : 2 * LANES] * (1.0 / SCALE_M),
        wide[:, :, 2 * LANES :] * (1.0 / SCALE_V),
        gradient,
    )
    mine = master[:, :ROW_NEW].astype(jnp.bfloat16).reshape(8, ROW_NEW * LANES)

    def linear(i_y, i_x, i_z, i_c):
        return ((i_y * 4 + i_x) * 4 + i_z) * 2 + i_c

    def moves(by, first):
        pairs = []
        for i_y in range(4):
            for i_x in range(4):
                for i_z in range(4):
                    for i_c in range(2):
                        along_x = (i_c == 0) == first
                        to_y = i_y if along_x else (i_y + by) % 4
                        to_x = (i_x + by) % 4 if along_x else i_x
                        pairs.append((linear(i_y, i_x, i_z, i_c), linear(to_y, to_x, i_z, i_c)))
        return pairs

    def turn(value, first):
        return [value] + [
            lax.ppermute(value, ("y", "x", "z", "c"), moves(by, first)) for by in TURNS[1:]
        ]

    mine, second = lax.optimization_barrier((mine, second))
    by_one = jnp.stack(turn(mine, True))
    held = turn(by_one, False)
    params = pl.pallas_call(
        place_kernel,
        out_shape=jax.ShapeDtypeStruct((16, 8, ROW_NEW * LANES), jnp.bfloat16),
        in_specs=[vmem] * 4,
        out_specs=vmem,
        compiler_params=pltpu.CompilerParams(vmem_limit_bytes=16 * 1024 * 1024),
    )(*held).reshape(128, ROW_NEW * LANES)

    ends = one_hot_dot(moved_ends, second)
    even = core == 0
    ends = ends.reshape(4, 2, RPAD, 3 * LANES)
    keep = jnp.where(even, ends[:, 0], ends[:, 1])
    got = lax.ppermute(jnp.where(even, ends[:, 1], ends[:, 0]), "c", [(0, 1), (1, 0)])
    both = jnp.stack([jnp.where(even, keep, got), jnp.where(even, got, keep)], axis=1)
    from_z = [lax.dynamic_index_in_dim(both, z, 0, keepdims=False)]
    for by in (2, 1, 3):
        leaving = lax.dynamic_index_in_dim(both, (z + by) % 4, 0, keepdims=False)
        from_z.append(lax.ppermute(leaving, "z", [(i, (i + by) % 4) for i in range(4)]))
    back = [from_z[3], from_z[1], from_z[2], from_z[0]]
    ends = lax.dynamic_slice_in_dim(jnp.stack(back + back), 3 - z, 4, 0)
    ends = ends.reshape(8, RPAD, 3 * LANES)
    outs = pl.pallas_call(
        owner_kernel,
        out_shape=(jax.ShapeDtypeStruct((1, SLOT, LANES), jnp.float32),) * 3,
        in_specs=[smem, vmem, vmem, vmem],
        out_specs=(vmem, vmem, vmem),
        scratch_shapes=[pltpu.VMEM((3, 2 * SLOT, LANES), jnp.float32)],
        compiler_params=pltpu.CompilerParams(vmem_limit_bytes=24 * 1024 * 1024),
    )(new_table.T, ends.astype(jnp.float32), block.astype(jnp.float32), grad)
    return (*outs, params)


def solution(mesh):
    fine = Mesh(mesh.devices.reshape(4, 4, 4, 2), ("y", "x", "z", "c"))
    parts = P(("y", "x", "z", "c"), None, None)
    return jax.shard_map(
        on_device,
        mesh=fine,
        in_specs=(parts, parts, parts, parts, P(), P(), P()),
        out_specs=(parts, parts, parts, P(None, ("z", "c"))),
        check_vma=False,
    )
```
